128 devices in a mesh: seq: 32 (over z_lo, x, y), batch: 4 (over z_hi, core).
Axes of the slice: x: 4, y: 4, z: 4 (z_hi: 2, z_lo: 2; z = z_hi * 2 + z_lo), core: 2. Of those that a mesh axis runs over, the one named last changes fastest.
Arguments:
- latent: bfloat16 [256, 256, 1152], P(('batch', 'seq')), parts along dimension 0, may hold values from -120 to 120, as said below
- modulation: float32 [24, 1152], P('batch'), parts along dimension 0, may hold values from -1.5 to 9
- w_spatial_qkv: bfloat16 [1152, 3456], replicated, may hold values from -0.1875 to 0.1875
- w_spatial_out: bfloat16 [1152, 1152], replicated, may hold values from -0.1875 to 0.1875
- w_temporal_qkv: bfloat16 [1152, 3456], replicated, may hold values from -0.1875 to 0.1875
- w_temporal_out: bfloat16 [1152, 1152], replicated, may hold values from -0.1875 to 0.1875
- cross_query: bfloat16 [1152, 1152], P('seq'), may hold values from -0.1875 to 0.1875
- cross_out: bfloat16 [1152, 1152], P('seq'), may hold values from -0.1875 to 0.1875
- text_keys: bfloat16 [480, 1152], P('batch'), parts along dimension 0, may hold values from -6 to 6
- text_values: bfloat16 [480, 1152], P('batch'), parts along dimension 0, may hold values from -6 to 6
- text_len: int32 [4], P('batch'), parts along dimension 0, may hold values from 30 to 120, as said below
Outputs:
- features_out: bfloat16 [256, 256, 1152], P(('batch', 'seq')), parts along dimension 0
The draws below stay inside these ranges and needn't reach their ends.
There are 4 independent parts, one for each index of `batch`. The reference program is written for one: setup_inputs(seed, part) draws one part's arguments, and reference() takes and returns one part's arrays. A program takes and returns all parts, laid end to end along the dimension named above; an argument that names none is the same for every part. Nothing has to cross between parts.
Inputs may be any that keep to these rules, and one draw needn't show every extreme that they name: `latent`: token features of order one; some rows may be far larger. Slots 0 to text_len - 1 hold the caption.
All inputs are finite; a program needn't handle non-finite values.
Results may differ from the reference program's by a relative error of at most 0.028.
The reference program's roundings to bfloat16 on the way count: a program that leaves them out, or rounds other values in their place, can miss the bound.
Values may be sent and summed in bfloat16 or wider, within the bound.
No kernel may reach another device: no remote copies, remote signals or barrier semaphores. Data moves between devices by JAX's collectives and lax.ppermute only.
A program may use at most 128 MiB of HBM per device.

```python
import jax
import jax.numpy as jnp
from jax import lax

D = 1152
H = 16
S = 256
L = 120
FRAMES = 64


def draw_latent(key, part):
    key = jax.random.fold_in(key, 11)
    first = jax.random.fold_in(key, 0)
    base = jnp.clip(jax.random.normal(first, (FRAMES, S, D), jnp.float32), -4.0, 4.0)
    return base.astype(jnp.bfloat16)


def draw_modulation(key, part):
    key = jax.random.fold_in(key, 23)
    first, second, third = jax.random.split(key, 3)
    gates = jax.random.uniform(third, (2, D), jnp.float32, 0.5, 1.5)
    shifts = jnp.clip(0.5 * jax.random.normal(first, (2, D), jnp.float32), -1.5, 1.5)
    scales = jnp.clip(0.3 * jax.random.normal(second, (2, D), jnp.float32), -0.9, 0.9)
    return jnp.stack([shifts[0], scales[0], gates[0], shifts[1], scales[1], gates[1]], axis=0)


def draw_text_keys(key, part):
    key = jax.random.fold_in(key, 37)
    values = jnp.clip(jax.random.normal(key, (L, D), jnp.float32), -5.0, 5.0)
    return values.astype(jnp.bfloat16)


def draw_text_len(key, part):
    key = jax.random.fold_in(key, 41)
    drawn = jax.random.randint(key, (1,), L // 4, L, jnp.int32)
    return jnp.where(part % 2 == 1, jnp.full((1,), L, jnp.int32), drawn)


def block_levels(own_key, extent, cuts, smallest, high):
    gain, own = 1.0, jax.random.fold_in(own_key, 6)
    for axis_at, shards_of in cuts:
        draws = jnp.exp(jax.random.uniform(jax.random.fold_in(own, axis_at), (shards_of,), jnp.float32, smallest / len(cuts), high / len(cuts)))
        gain = gain * jnp.repeat(draws, extent[axis_at] // shards_of).reshape([-1 if axis == axis_at else 1 for axis in range(len(extent))])
    return gain


def bell_draw(own_key, extent, deviation, most, shards=(), kind=jnp.bfloat16):
    entries = jax.random.normal(own_key, extent, jnp.float32) * deviation
    if len(shards) > 0:
        entries = block_levels(own_key, extent, shards, -0.22, 0.18) * entries
    return jnp.clip(entries, min=-most, max=most).astype(kind)


def setup_inputs(seed: int = 0, part: int = 0) -> dict:
    streams_of = jax.random.split(jax.random.key(seed), 12)
    own_keys = jax.random.split(jax.random.fold_in(streams_of[11], part), 12)
    return {
        "latent": draw_latent(jax.random.fold_in(jax.random.fold_in(streams_of[11], part), 71), part),
        "modulation": draw_modulation(jax.random.fold_in(jax.random.fold_in(streams_of[11], part), 71), part),
        "w_spatial_qkv": bell_draw(streams_of[2], (D, 3 * D), D ** -0.5, 0.1875),
        "w_spatial_out": bell_draw(streams_of[3], (D, D), D ** -0.5, 0.1875),
        "w_temporal_qkv": bell_draw(streams_of[4], (D, 3 * D), D ** -0.5, 0.1875),
        "w_temporal_out": bell_draw(streams_of[5], (D, D), D ** -0.5, 0.1875),
        "cross_query": bell_draw(streams_of[6], (D, D), D ** -0.5, 0.1875, ((0, 32),)),
        "cross_out": bell_draw(streams_of[7], (D, D), D ** -0.5, 0.1875, ((0, 32),)),
        "text_keys": draw_text_keys(jax.random.fold_in(jax.random.fold_in(streams_of[11], part), 71), part),
        "text_values": bell_draw(own_keys[9], (L, D), 1.0, 6.0),
        "text_len": draw_text_len(jax.random.fold_in(jax.random.fold_in(streams_of[11], part), 71), part),
    }


def norm_mod(rows, shift, scale):
    values = rows.astype(jnp.float32)
    mean = lax.optimization_barrier(jnp.mean(values, axis=-1, keepdims=True))
    centered = values - mean
    var = lax.optimization_barrier(jnp.mean(centered * centered, axis=-1, keepdims=True))
    return (centered * lax.rsqrt(var + 1e-06) * (1.0 + scale) + shift).astype(jnp.bfloat16)

def attend(query, keys, values, valid):
    nq = query.shape[0]
    width = query.shape[1]
    head_size = width // H
    q4 = query.reshape(nq, H, head_size).astype(jnp.float32)
    k4 = keys.reshape(keys.shape[0], H, head_size).astype(jnp.float32)
    v4 = values.reshape(values.shape[0], H, head_size).astype(jnp.float32)
    scores = jnp.einsum('qhd,khd->hqk', q4, k4) / jnp.sqrt(jnp.float32(head_size))
    if valid is not None:
        scores = jnp.where(valid[None, None, :], scores, jnp.float32(-1e+30))
    top = lax.optimization_barrier(jnp.max(scores, axis=-1, keepdims=True))
    expo = jnp.exp(scores - top)
    weights = (expo / lax.optimization_barrier(jnp.sum(expo, axis=-1, keepdims=True))).astype(jnp.bfloat16)
    mixed = jnp.einsum('hqk,khd->qhd', weights.astype(jnp.float32), v4)
    return mixed.reshape(nq, width).astype(jnp.bfloat16)

def self_block(rows, modulation, w_qkv, w_out, first):
    normed = norm_mod(rows, modulation[first], modulation[first + 1])
    qkv = jnp.dot(normed, w_qkv, preferred_element_type=jnp.float32).astype(jnp.bfloat16)
    width = rows.shape[1]
    mixed = attend(qkv[:, :width], qkv[:, width:2 * width], qkv[:, 2 * width:], None)
    proj = jnp.dot(mixed, w_out, preferred_element_type=jnp.float32)
    return (rows.astype(jnp.float32) + modulation[first + 2] * proj).astype(jnp.bfloat16)

def reference(latent, modulation, w_spatial_qkv, w_spatial_out, w_temporal_qkv, w_temporal_out, cross_query, cross_out, text_keys, text_values, text_len):
    after_spatial = lax.map(lambda frame: self_block(frame, modulation, w_spatial_qkv, w_spatial_out, 0), latent)
    by_position = jnp.swapaxes(after_spatial, 0, 1)
    after_temporal = lax.map(lambda column: self_block(column, modulation, w_temporal_qkv, w_temporal_out, 3), by_position)
    after_temporal = jnp.swapaxes(after_temporal, 0, 1)
    valid = jnp.arange(text_keys.shape[0], dtype=jnp.int32) < text_len[0]

    def cross_frame(frame):
        query = jnp.dot(frame, cross_query, preferred_element_type=jnp.float32).astype(jnp.bfloat16)
        mixed = attend(query, text_keys, text_values, valid)
        proj = jnp.dot(mixed, cross_out, preferred_element_type=jnp.float32)
        return (frame.astype(jnp.float32) + proj).astype(jnp.bfloat16)
    return lax.map(cross_frame, after_temporal)
```

```python
import jax
import jax.numpy as jnp
from jax import lax
from jax.sharding import Mesh, PartitionSpec as P

H = 16
SEQ = ("z_lo", "x", "y")
ALL = ("z_hi", "core", "z_lo", "x", "y")


def norm_mod(rows, shift, scale):
    values = rows.astype(jnp.float32)
    mean = jnp.mean(values, axis=-1, keepdims=True)
    centered = values - mean
    var = jnp.mean(centered * centered, axis=-1, keepdims=True)
    return (centered * lax.rsqrt(var + 1e-06) * (1.0 + scale) + shift).astype(jnp.bfloat16)


def softmax_weights(scores):
    top = jnp.max(scores, axis=-1, keepdims=True)
    expo = jnp.exp(scores - top)
    return (expo / jnp.sum(expo, axis=-1, keepdims=True)).astype(jnp.bfloat16)


def within_frames(qkv):
    frames, tokens, triple = qkv.shape
    width = triple // 3
    head_size = width // H
    split = qkv.reshape(frames, tokens, 3, H, head_size)
    scores = jnp.einsum(
        "fqhd,fkhd->fhqk", split[:, :, 0], split[:, :, 1], preferred_element_type=jnp.float32
    )
    weights = softmax_weights(scores / jnp.sqrt(jnp.float32(head_size)))
    mixed = jnp.einsum(
        "fhqk,fkhd->fqhd", weights, split[:, :, 2], preferred_element_type=jnp.float32
    )
    return mixed.reshape(frames, tokens, width).astype(jnp.bfloat16)


def across_frames(qkv):
    frames, places, triple = qkv.shape
    width = triple // 3
    head_size = width // H
    split = qkv.reshape(frames, places, 3, H, head_size)
    scores = jnp.einsum(
        "qphd,kphd->phqk", split[:, :, 0], split[:, :, 1], preferred_element_type=jnp.float32
    )
    weights = softmax_weights(scores / jnp.sqrt(jnp.float32(head_size)))
    mixed = jnp.einsum(
        "phqk,kphd->qphd", weights, split[:, :, 2], preferred_element_type=jnp.float32
    )
    return mixed.reshape(frames, places, width).astype(jnp.bfloat16)


def project(rows, weight):
    lead = rows.shape[:-1]
    flat = rows.reshape(-1, rows.shape[-1])
    return jnp.dot(flat, weight, preferred_element_type=jnp.float32).reshape(
        lead + (weight.shape[1],)
    )


def gather_cross(cross_query, cross_out):
    core = lax.axis_index("core")
    mine = jnp.where(core == 0, cross_query, cross_out)
    copies = jnp.broadcast_to(mine[None], (32,) + mine.shape)
    whole = lax.all_to_all(copies, SEQ, split_axis=0, concat_axis=0, tiled=False)
    other = lax.ppermute(whole, "core", [(0, 1), (1, 0)])
    query = jnp.where(core == 0, whole, other).reshape(-1, mine.shape[1])
    out = jnp.where(core == 0, other, whole).reshape(-1, mine.shape[1])
    return query, out


def body(
    latent,
    modulation,
    w_spatial_qkv,
    w_spatial_out,
    w_temporal_qkv,
    w_temporal_out,
    cross_query,
    cross_out,
    text_keys,
    text_values,
    text_len,
):
    width = latent.shape[2]
    whole_query, whole_out = gather_cross(cross_query, cross_out)
    spatial_in = norm_mod(latent, modulation[0], modulation[1])
    spatial_qkv = project(spatial_in, w_spatial_qkv).astype(jnp.bfloat16)
    spatial_ctx = within_frames(spatial_qkv)
    after_spatial = (
        latent.astype(jnp.float32) + modulation[2] * project(spatial_ctx, w_spatial_out)
    ).astype(jnp.bfloat16)
    after_spatial = lax.all_to_all(after_spatial, SEQ, split_axis=1, concat_axis=0, tiled=True)
    temporal_in = norm_mod(after_spatial, modulation[3], modulation[4])
    temporal_qkv = project(temporal_in, w_temporal_qkv).astype(jnp.bfloat16)
    temporal_ctx = across_frames(temporal_qkv)
    after_temporal = (
        after_spatial.astype(jnp.float32) + modulation[5] * project(temporal_ctx, w_temporal_out)
    ).astype(jnp.bfloat16)
    flat_rows = after_temporal.reshape(-1, width)
    cross_q = project(flat_rows, whole_query).astype(jnp.bfloat16)
    head_size = width // H
    slots = text_keys.shape[0]
    valid = jnp.arange(slots, dtype=jnp.int32) < text_len[0]
    q_heads = cross_q.reshape(-1, H, head_size)
    scores = jnp.einsum(
        "thd,lhd->htl",
        q_heads,
        text_keys.reshape(slots, H, head_size),
        preferred_element_type=jnp.float32,
    )
    scores = jnp.where(
        valid[None, None, :], scores / jnp.sqrt(jnp.float32(head_size)), jnp.float32(-1e30)
    )
    weights = softmax_weights(scores)
    cross_ctx = jnp.einsum(
        "htl,lhd->thd",
        weights,
        text_values.reshape(slots, H, head_size),
        preferred_element_type=jnp.float32,
    )
    cross_ctx = cross_ctx.reshape(-1, width).astype(jnp.bfloat16)
    result = flat_rows.astype(jnp.float32) + project(cross_ctx, whole_out)
    result = result.reshape(after_temporal.shape).astype(jnp.bfloat16)
    return lax.all_to_all(result, SEQ, split_axis=0, concat_axis=1, tiled=True)


def solution(mesh):
    fine = Mesh(mesh.devices.reshape(2, 4, 4, 2, 2), ("z_lo", "x", "y", "z_hi", "core"))
    part = ("z_hi", "core")
    placed = (
        P(ALL, None, None),
        P(part, None),
        P(),
        P(),
        P(),
        P(),
        P(SEQ, None),
        P(SEQ, None),
        P(part, None),
        P(part, None),
        P(part),
    )
    return jax.shard_map(
        body, mesh=fine, in_specs=placed, out_specs=P(ALL, None, None), check_vma=False
    )
```

```python
import functools
import jax
import jax.numpy as jnp
import numpy as np
from jax import lax
from jax.experimental import pallas as pl
from jax.experimental.pallas import tpu as pltpu
from jax.sharding import Mesh, PartitionSpec as P

H = 16
HEAD = 72
LANES = 9
D = 1152
S = 256
T = 512
WIN = 256
SLOTS = 128
BLOCK = 144
SEQ = ("z_lo", "x", "y")
ALL = ("z_hi", "core", "z_lo", "x", "y")
EXP_SCALE = float(np.log2(np.e) / np.sqrt(72.0))
CHUNK = 768
F32 = jnp.float32
BF16 = jnp.bfloat16
NT = (((1,), (1,)), ((), ()))


def mm(a, b):
    return jnp.dot(a, b, preferred_element_type=F32)


def mm_nt(a, b):
    return lax.dot_general(a, b, NT, preferred_element_type=F32)


def window(head):
    return min(HEAD * head // 128 * 128, D - WIN)


def head_mask(head):
    lane = lax.broadcasted_iota(jnp.int32, (1, WIN), 1) + window(head)
    inside = (lane >= HEAD * head) & (lane < HEAD * head + HEAD)
    return jnp.where(inside, 1.0, 0.0).astype(BF16)


def identity(n):
    rows = lax.broadcasted_iota(jnp.int32, (n, n), 0)
    cols = lax.broadcasted_iota(jnp.int32, (n, n), 1)
    return jnp.where(rows == cols, 1.0, 0.0).astype(BF16)


def norm_mod(values, shift, scale):
    mean = jnp.mean(values, axis=-1, keepdims=True)
    centered = values - mean
    var = jnp.mean(centered * centered, axis=-1, keepdims=True)
    return (centered * lax.rsqrt(var + 1e-06) * (1.0 + scale) + shift).astype(BF16)


def column_chunks(width, chunk):
    return [(at, min(chunk, width - at)) for at in range(0, width, chunk)]


def fetch(src, dst, sems, chunk):
    copies = []
    for n, (at, size) in enumerate(column_chunks(src.shape[1], chunk)):
        cols = pl.ds(at, size)
        copies.append(pltpu.make_async_copy(src.at[:, cols], dst.at[:, cols], sems.at[n]))
    for copy in copies:
        copy.start()
    return copies


def transpose_into(dst, eye, src, at):
    for lo, size in column_chunks(D, WIN):
        dst[lo : lo + size, :] = mm_nt(eye[:size, :size], src(lo, size)).astype(dst.dtype)


def project_qkv(xn, w_vm, copies, qkv):
    for copy, (at, size) in zip(copies, column_chunks(3 * D, CHUNK)):
        copy.wait()
        for lo in range(0, xn.shape[0], S):
            rows = slice(lo, lo + S)
            qkv[rows, at : at + size] = mm(xn[rows, :], w_vm[:, at : at + size]).astype(BF16)


def softmax_cols(scores):
    top = jnp.max(scores, axis=0, keepdims=True)
    expo = jnp.exp2(scores * EXP_SCALE - top * EXP_SCALE)
    return expo, jnp.sum(expo, axis=0, keepdims=True)


def attend_full(scores):
    expo, total = softmax_cols(scores)
    return expo.astype(BF16), total


def attend_blocks(scores):
    lane = lax.broadcasted_iota(jnp.int32, (64, 128), 1)
    low = lane < 64
    left = jnp.where(low, scores[0:64, :128], scores[64:128, :128])
    right = jnp.where(low, scores[128:192, 128:], scores[192:256, 128:])
    le, lt = softmax_cols(left)
    re, rt = softmax_cols(right)
    zero = jnp.zeros((64, 128), F32)
    wide = jnp.concatenate(
        [
            jnp.concatenate([jnp.where(low, le, zero), zero], 1),
            jnp.concatenate([jnp.where(low, zero, le), zero], 1),
            jnp.concatenate([zero, jnp.where(low, re, zero)], 1),
            jnp.concatenate([zero, jnp.where(low, zero, re)], 1),
        ],
        0,
    )
    return wide.astype(BF16), jnp.concatenate([lt, rt], 1)


def self_attention(qkv, v_t, ctx_t, ctx, weigh):
    eye = identity(WIN)

    def group(g, carry):
        rows = pl.ds(g * S, S) if isinstance(g, int) else pl.ds(pl.multiple_of(g * S, S), S)
        transpose_into(v_t, eye, lambda lo, size: qkv[rows, 2 * D + lo : 2 * D + lo + size], 0)
        for head in range(H):
            at = window(head)
            query = qkv[rows, at : at + WIN] * head_mask(head)
            keys = qkv[rows, D + at : D + at + WIN]
            weights, total = weigh(mm_nt(keys, query))
            lo = head * HEAD
            mixed = mm(v_t[lo : lo + HEAD, :].astype(BF16), weights)
            ctx_t[lo : lo + HEAD, :] = mixed * (1.0 / total)
        ctx[rows, :] = mm_nt(eye, ctx_t[...].astype(BF16)).astype(BF16)
        return carry

    if qkv.shape[0] == S:
        group(0, 0)
    else:
        lax.fori_loop(0, qkv.shape[0] // S, group, 0)


def spatial_kernel(frame, *refs):
    if frame == 0:
        first, (lat, mod, w_hbm, wo_hbm, out, *scratch) = None, refs
    else:
        first, lat, mod, w_hbm, wo_hbm, out, *scratch = refs
    xn, w_vm, wo_vm, qkv, v_t, ctx_t, ctx, proj, sems, osem = scratch
    copies = fetch(w_hbm, w_vm, sems, CHUNK)
    out_copy = pltpu.make_async_copy(wo_hbm, wo_vm, osem)
    out_copy.start()
    shift, scale, gate = mod[0:1, :], mod[1:2, :], mod[2:3, :]

    def norm_rows(i, carry):
        rows = pl.ds(pl.multiple_of(i * 32, 32), 32)
        xn[rows, :] = norm_mod(lat[frame, rows, :].astype(F32), shift, scale)
        return carry

    lax.fori_loop(0, S // 32, norm_rows, 0)
    project_qkv(xn, w_vm, copies, qkv)
    self_attention(qkv, v_t, ctx_t, ctx, attend_full)
    out_copy.wait()
    proj[...] = mm(ctx[...], wo_vm[...])

    def finish(i, carry):
        rows = pl.ds(pl.multiple_of(i * 32, 32), 32)
        value = lat[frame, rows, :].astype(F32) + gate * proj[rows, :]
        if frame == 0:
            out[rows, :] = value.astype(BF16)
        else:
            parts = [first[rows, :].astype(F32).reshape(4, 8, D), value.reshape(4, 8, D)]
            out[pl.ds(pl.multiple_of(i * 4, 4), 4)] = jnp.concatenate(parts, axis=1).astype(BF16)
        return carry

    lax.fori_loop(0, S // 32, finish, 0)


def vmem():
    return pl.BlockSpec(memory_space=pltpu.VMEM)


def hbm():
    return pl.BlockSpec(memory_space=pl.ANY)


def block_scratch(rows):
    n = len(column_chunks(3 * D, CHUNK))
    return [
        pltpu.VMEM((rows, D), BF16),
        pltpu.VMEM((D, 3 * D), BF16),
        pltpu.VMEM((D, D), BF16),
        pltpu.VMEM((rows, 3 * D), BF16),
        pltpu.VMEM((D, S), F32),
        pltpu.VMEM((D, S), F32),
        pltpu.VMEM((rows, D), BF16),
        pltpu.VMEM((rows, D), F32),
        pltpu.SemaphoreType.DMA((n,)),
        pltpu.SemaphoreType.DMA,
    ]


PARAMS = pltpu.CompilerParams(vmem_limit_bytes=48 * 1024 * 1024)


def spatial(frame, first, lat, mod, w, wo):
    shape = (S, D) if frame == 0 else (32, 16, D)
    lead = [] if frame == 0 else [first]
    return pl.pallas_call(
        functools.partial(spatial_kernel, frame),
        out_shape=jax.ShapeDtypeStruct(shape, BF16),
        in_specs=[vmem()] * len(lead) + [vmem(), vmem(), hbm(), hbm()],
        out_specs=vmem(),
        scratch_shapes=block_scratch(S),
        compiler_params=PARAMS,
        cost_estimate=pl.CostEstimate(flops=4_000_000_000, bytes_accessed=13_000_000, transcendentals=1_000_000),
        name=f"spatial_{frame}",
    )(*lead, lat, mod, w, wo)


def temporal_kernel(x, mod, w_hbm, wo_hbm, out, xn, w_vm, wo_vm, qkv, v_t, ctx_t, ctx, proj, sems, osem, wide):
    copies = fetch(w_hbm, w_vm, sems, CHUNK)
    out_copy = pltpu.make_async_copy(wo_hbm, wo_vm, osem)
    out_copy.start()
    shift, scale, gate = mod[3:4, :], mod[4:5, :], mod[5:6, :]

    def widen(i, carry):
        value = x[i].astype(F32)
        for j in range(LANES):
            wide[j, pl.ds(pl.multiple_of(i * 16, 16), 16), :] = value[:, j * 128 : j * 128 + 128]
        return carry

    lax.fori_loop(0, 32, widen, 0, unroll=4)

    def norm_rows(i, carry):
        p, q = i // 2, i % 2
        picked = pl.ds(q * 256 + p, 32, stride=8)
        values = jnp.concatenate([wide[j, picked, :] for j in range(LANES)], axis=1)
        rows = pl.ds(pl.multiple_of(i * 32, 32), 32)
        out[rows, :] = values.astype(BF16)
        xn[rows, :] = norm_mod(values, shift, scale)
        return carry

    lax.fori_loop(0, 16, norm_rows, 0)
    project_qkv(xn, w_vm, copies, qkv)
    self_attention(qkv, v_t, ctx_t, ctx, attend_blocks)
    out_copy.wait()
    for f in range(2):
        rows = slice(f * S, f * S + S)
        proj[rows, :] = mm(ctx[rows, :], wo_vm[...])

    def finish(i, carry):
        rows = pl.ds(pl.multiple_of(i * 32, 32), 32)
        out[rows, :] = (out[rows, :].astype(F32) + gate * proj[rows, :]).astype(BF16)
        return carry

    lax.fori_loop(0, 16, finish, 0)


def temporal(x, mod, w, wo):
    return pl.pallas_call(
        temporal_kernel,
        out_shape=jax.ShapeDtypeStruct((T, D), BF16),
        in_specs=[vmem(), vmem(), hbm(), hbm()],
        out_specs=vmem(),
        scratch_shapes=block_scratch(T) + [pltpu.VMEM((LANES, T, 128), F32)],
        compiler_params=PARAMS,
        cost_estimate=pl.CostEstimate(flops=8_000_000_000, bytes_accessed=13_000_000, transcendentals=600_000),
        name="temporal",
    )(x, mod, w, wo)


def cross_kernel(place, x, keys, values, *refs):
    pieces, (out, w_vm, query, v_t, ctx_t, ctx, wide, sems) = refs[:10], refs[10:]
    length, core, z_lo, x_at = place[0], place[1], place[2], place[3]

    def put(which, src, z, x_from):
        rows = pl.ds(pl.multiple_of(z * (D // 2) + x_from * BLOCK, 16), BLOCK)
        pltpu.make_async_copy(src, w_vm.at[which, rows, :], sems.at[which]).start()

    left, right, far = (x_at + 3) % 4, (x_at + 1) % 4, (x_at + 2) % 4
    for own in range(2):
        which = core if own == 0 else 1 - core
        here, from_left, from_right, far_same, far_other = pieces[5 * own : 5 * own + 5]
        for n, z in enumerate((z_lo, 1 - z_lo)):
            put(which, here.at[n], z, x_at)
            put(which, from_left.at[n], z, left)
            put(which, from_right.at[n], z, right)
        put(which, far_same, z_lo, far)
        put(which, far_other, 1 - z_lo, far)

    def whole(which):
        pltpu.make_async_copy(w_vm.at[which], w_vm.at[which], sems.at[which]).wait()

    eye = identity(WIN)
    for lo, size in column_chunks(D, WIN):
        v_t[lo : lo + size, :] = mm_nt(eye[:size, :size], values[:, lo : lo + size])
    whole(0)
    for f in range(2):
        rows = slice(f * S, f * S + S)
        query[rows, :] = mm(x[rows, :], w_vm[0]).astype(BF16)
    valid = lax.broadcasted_iota(jnp.int32, (SLOTS, S), 0) < length

    def group(g, carry):
        rows = pl.ds(pl.multiple_of(g * S, S), S)
        for head in range(H):
            at = window(head)
            masked = keys[:, at : at + WIN] * head_mask(head)
            scores = mm_nt(masked, query[rows, at : at + WIN])
            expo, total = softmax_cols(jnp.where(valid, scores, -1e30))
            lo = head * HEAD
            mixed = mm(v_t[lo : lo + HEAD, :].astype(BF16), expo.astype(BF16))
            ctx_t[lo : lo + HEAD, :] = mixed * (1.0 / total)
        ctx[rows, :] = mm_nt(eye, ctx_t[...].astype(BF16)).astype(BF16)
        return carry

    lax.fori_loop(0, 2, group, 0)
    whole(1)
    for f in range(2):
        rows = slice(f * S, f * S + S)
        ctx_rows = mm(ctx[rows, :], w_vm[1])
        value = x[rows, :].astype(F32) + ctx_rows
        for p in range(4):
            for j in range(LANES):
                wide[j, pl.ds(f * 4 + p, 64, stride=8), :] = value[p * 64 : p * 64 + 64, j * 128 : j * 128 + 128]

    def narrow(i, carry):
        rows = pl.ds(pl.multiple_of(i * 16, 16), 16)
        out[i] = jnp.concatenate([wide[j, rows, :] for j in range(LANES)], axis=1).astype(BF16)
        return carry

    lax.fori_loop(0, 32, narrow, 0, unroll=4)


def cross(place, x, keys, values, pieces):
    return pl.pallas_call(
        cross_kernel,
        out_shape=jax.ShapeDtypeStruct((32, 16, D), BF16),
        in_specs=[pl.BlockSpec(memory_space=pltpu.SMEM), vmem(), vmem(), vmem()] + [hbm()] * len(pieces),
        out_specs=vmem(),
        scratch_shapes=[
            pltpu.VMEM((2, D, D), BF16),
            pltpu.VMEM((T, D), BF16),
            pltpu.VMEM((D, SLOTS), F32),
            pltpu.VMEM((D, S), F32),
            pltpu.VMEM((T, D), BF16),
            pltpu.VMEM((LANES, T, 128), F32),
            pltpu.SemaphoreType.DMA((2,)),
        ],
        compiler_params=PARAMS,
        cost_estimate=pl.CostEstimate(flops=4_000_000_000, bytes_accessed=8_000_000, transcendentals=1_000_000),
        name="cross",
    )(place, x, keys, values, *pieces)


def shift(array, axis, by, size):
    return lax.ppermute(array, axis, [(i, (i + by) % size) for i in range(size)])


def gather_first(cross_query, cross_out):
    mine = jnp.where(lax.axis_index("core") == 0, cross_query, cross_out)

    def over_yz(by_z, by):
        pairs = [
            (z * 4 + y, (z + by_z) % 2 * 4 + (y + by) % 4) for z in range(2) for y in range(4)
        ]
        return lax.ppermute(mine, ("z_lo", "y"), pairs)

    found = []
    for by_z in range(2):
        rows = [mine if (by_z, by) == (0, 0) else over_yz(by_z, by) for by in (3, 2, 1, 0)]
        found.append(jnp.stack(rows + rows[:3]))
    found = jnp.stack(found)
    start = 3 - lax.axis_index("y")
    ordered = lax.dynamic_slice_in_dim(found, start, 4, axis=1)
    return ordered.reshape(2, BLOCK, D)


def gather_second(here):
    left = shift(here, "x", 1, 4)
    right = shift(here, "x", -1, 4)
    far_same = shift(left[0], "x", 1, 4)
    far_other = shift(right[1], "x", -1, 4)
    pieces = [here, left, right, far_same, far_other]
    return pieces + [shift(piece, "core", 1, 2) for piece in pieces]


def body(
    latent,
    modulation,
    w_spatial_qkv,
    w_spatial_out,
    w_temporal_qkv,
    w_temporal_out,
    cross_query,
    cross_out,
    text_keys,
    text_values,
    text_len,
):
    near = gather_first(cross_query, cross_out)
    first = spatial(0, None, latent, modulation, w_spatial_qkv, w_spatial_out)
    near, first = lax.optimization_barrier((near, first))
    pieces = gather_second(near)
    after_spatial = spatial(1, first, latent, modulation, w_spatial_qkv, w_spatial_out)
    placed = lax.all_to_all(after_spatial, SEQ, split_axis=0, concat_axis=0, tiled=True)
    after_temporal = temporal(placed, modulation, w_temporal_qkv, w_temporal_out)
    place = jnp.stack(
        [text_len[0], lax.axis_index("core"), lax.axis_index("z_lo"), lax.axis_index("x")]
    ).astype(jnp.int32)
    fill = ((0, SLOTS - text_keys.shape[0]), (0, 0))
    keys, values = jnp.pad(text_keys, fill), jnp.pad(text_values, fill)
    result = cross(place, after_temporal, keys, values, pieces)
    returned = lax.all_to_all(result, SEQ, split_axis=0, concat_axis=0, tiled=True)
    return returned.reshape(32, 2, 8, D).transpose(1, 0, 2, 3).reshape(2, S, D)


def solution(mesh):
    fine = Mesh(mesh.devices.reshape(2, 4, 4, 2, 2), ("z_lo", "x", "y", "z_hi", "core"))
    part = ("z_hi", "core")
    placed = (
        P(ALL, None, None),
        P(part, None),
        P(),
        P(),
        P(),
        P(),
        P(SEQ, None),
        P(SEQ, None),
        P(part, None),
        P(part, None),
        P(part),
    )
    return jax.shard_map(
        body, mesh=fine, in_specs=placed, out_specs=P(ALL, None, None), check_vma=False
    )
```

```python
import jax
import jax.numpy as jnp
import numpy as np
from jax import lax
from jax.experimental import pallas as pl
from jax.experimental.pallas import tpu as pltpu
from jax.sharding import Mesh, PartitionSpec as P

H = 16
HEAD = 72
LANES = 9
D = 1152
S = 256
T = 512
WIN = 256
SLOTS = 128
BLOCK = 144
CUT = 80
CHUNK = 512
EXP_SCALE = float(np.log2(np.e) / np.sqrt(72.0))
F32 = jnp.float32
BF16 = jnp.bfloat16
NT = (((1,), (1,)), ((), ()))
SEQ = ("z_lo", "x", "y")
ALL = ("z_hi", "core", "z_lo", "x", "y")


def mm(a, b):
    return jnp.dot(a, b, preferred_element_type=F32)


def mm_nt(a, b):
    return lax.dot_general(a, b, NT, preferred_element_type=F32)


def window(head):
    return min(HEAD * head // 128 * 128, D - WIN)


def lane_mask(head, at, size):
    lane = lax.broadcasted_iota(jnp.int32, (1, size), 1) + at
    inside = (lane >= HEAD * head) & (lane < HEAD * head + HEAD)
    return jnp.where(inside, 1.0, 0.0).astype(BF16)


def heads_of(at, size):
    return [h for h in range(H) if h * HEAD < at + size and h * HEAD + HEAD > at]


def identity(n):
    rows = lax.broadcasted_iota(jnp.int32, (n, n), 0)
    cols = lax.broadcasted_iota(jnp.int32, (n, n), 1)
    return jnp.where(rows == cols, 1.0, 0.0).astype(BF16)


def norm_mod(values, shift, scale):
    mean = jnp.mean(values, axis=-1, keepdims=True)
    centered = values - mean
    var = jnp.mean(centered * centered, axis=-1, keepdims=True)
    return (centered * lax.rsqrt(var + 1e-06) * (1.0 + scale) + shift).astype(BF16)


def column_chunks(width, chunk):
    return [(at, min(chunk, width - at)) for at in range(0, width, chunk)]


def halves(body):
    def step(g, carry):
        body(g, pl.ds(pl.multiple_of(g * S, S), S))
        return carry

    lax.fori_loop(0, 2, step, 0)


def project_qkv(xn, w, qkv):
    for at, size in column_chunks(3 * D, CHUNK):
        for rows in (slice(0, S), slice(S, T)):
            qkv[rows, at : at + size] = mm(xn[rows, :], w[:, at : at + size]).astype(BF16)


def softmax_rows(scores):
    top = jnp.max(scores, axis=1, keepdims=True)
    expo = jnp.exp2(scores * EXP_SCALE - top * EXP_SCALE)
    return (expo * (1.0 / jnp.sum(expo, axis=1, keepdims=True))).astype(BF16)


def softmax_cols(scores):
    top = jnp.max(scores, axis=0, keepdims=True)
    expo = jnp.exp2(scores * EXP_SCALE - top * EXP_SCALE)
    return expo, 1.0 / jnp.sum(expo, axis=0, keepdims=True)


def softmax_blocks(scores):
    low = lax.broadcasted_iota(jnp.int32, (64, 128), 1) < 64
    left, over_left = softmax_cols(jnp.where(low, scores[0:64, :128], scores[64:128, :128]))
    right, over_right = softmax_cols(jnp.where(low, scores[128:192, 128:], scores[192:256, 128:]))
    zero = jnp.zeros((64, 128), F32)
    wide = jnp.concatenate(
        [
            jnp.concatenate([jnp.where(low, left, zero), zero], 1),
            jnp.concatenate([jnp.where(low, zero, left), zero], 1),
            jnp.concatenate([zero, jnp.where(low, right, zero)], 1),
            jnp.concatenate([zero, jnp.where(low, zero, right)], 1),
        ],
        0,
    )
    return wide.astype(BF16), jnp.concatenate([over_left, over_right], 1)


def spatial_kernel(lat, mod, w, wo, out, xn, qkv, weights, ctx):
    shift, scale, gate = mod[0:1, :], mod[1:2, :], mod[2:3, :]

    def norm_rows(i, carry):
        rows = pl.ds(pl.multiple_of(i * 64, 64), 64)
        xn[rows, :] = norm_mod(lat[rows, :].astype(F32), shift, scale)
        return carry

    lax.fori_loop(0, T // 64, norm_rows, 0, unroll=2)
    project_qkv(xn, w, qkv)

    def attend(g, rows):
        for head in range(H):
            at = window(head)
            query = qkv[rows, at : at + WIN] * lane_mask(head, at, WIN)
            weights[head] = softmax_rows(mm_nt(query, qkv[rows, D + at : D + at + WIN]))
        for at, size in column_chunks(D, WIN):
            values = qkv[rows, 2 * D + at : 2 * D + at + size]
            mixed = 0
            for head in heads_of(at, size):
                mixed = mixed + mm(weights[head], values * lane_mask(head, at, size))
            ctx[rows, at : at + size] = mixed.astype(BF16)

    halves(attend)
    for at, size in column_chunks(D, WIN):
        cols = slice(at, at + size)
        parts = []
        for rows in (slice(0, S), slice(S, T)):
            value = lat[rows, cols].astype(F32) + gate[:, cols] * mm(ctx[rows, :], wo[:, cols])
            parts.append(value.reshape(32, 8, size))
        out[:, :, cols] = jnp.concatenate(parts, axis=1).astype(BF16)


def temporal_kernel(x, mod, w, wo, out, xn, qkv, weights, ctx, rest, over, v_t, ctx_t, wide):
    shift, scale, gate = mod[3:4, :], mod[4:5, :], mod[5:6, :]

    def widen(i, carry):
        value = x[i].astype(F32)
        for j in range(LANES):
            wide[j, pl.ds(pl.multiple_of(i * 16, 16), 16), :] = value[:, j * 128 : j * 128 + 128]
        return carry

    lax.fori_loop(0, 32, widen, 0, unroll=4)

    def norm_rows(p, carry):
        picked = pl.ds(p, 64, stride=8)
        values = jnp.concatenate([wide[j, picked, :] for j in range(LANES)], axis=1)
        rows = pl.ds(pl.multiple_of(p * 64, 64), 64)
        rest[rows, :] = values.astype(BF16)
        xn[rows, :] = norm_mod(values, shift, scale)
        return carry

    lax.fori_loop(0, 8, norm_rows, 0, unroll=2)
    project_qkv(xn, w, qkv)
    eye = identity(WIN)

    def attend(g, rows):
        for at, size in column_chunks(D, WIN):
            v_t[at : at + size, :] = mm_nt(eye[:size, :size], qkv[rows, 2 * D + at : 2 * D + at + size])
        for head in range(H):
            at = window(head)
            query = qkv[rows, at : at + WIN] * lane_mask(head, at, WIN)
            weights[head], over[head] = softmax_blocks(mm_nt(qkv[rows, D + at : D + at + WIN], query))
        for head in range(H):
            mine = slice(head * HEAD, head * HEAD + HEAD)
            ctx_t[mine, :] = mm(v_t[mine, :].astype(BF16), weights[head]) * over[head]
        ctx[rows, :] = mm_nt(eye, ctx_t[...].astype(BF16)).astype(BF16)

    halves(attend)
    for at, size in column_chunks(D, WIN):
        cols = slice(at, at + size)
        for g in range(2):
            rows = slice(g * S, g * S + S)
            value = rest[rows, cols].astype(F32) + gate[:, cols] * mm(ctx[rows, :], wo[:, cols])
            for p in range(4):
                for j in range(size // 128):
                    piece = value[p * 64 : p * 64 + 64, j * 128 : j * 128 + 128]
                    wide[at // 128 + j, pl.ds(g * 4 + p, 64, stride=8), :] = piece

    def narrow(i, carry):
        rows = pl.ds(pl.multiple_of(i * 16, 16), 16)
        out[i] = jnp.concatenate([wide[j, rows, :] for j in range(LANES)], axis=1).astype(BF16)
        return carry

    lax.fori_loop(0, 32, narrow, 0, unroll=4)


def cross_kernel(place, x, keys, values, *refs):
    pieces, (out, w, query, weights, over, v_t, ctx_t, ctx, sems) = refs[:10], refs[10:]
    length, core, z_lo, x_at = place[0], place[1], place[2], place[3]

    def put(which, src, z, x_from, skip, size):
        row = pl.multiple_of(z * (D // 2) + x_from * BLOCK + skip, 16)
        pltpu.make_async_copy(src, w.at[which, pl.ds(row, size), :], sems.at[which]).start()

    left, right, far = (x_at + 3) % 4, (x_at + 1) % 4, (x_at + 2) % 4
    for own in range(2):
        which = core if own == 0 else 1 - core
        here, from_left, from_right, far_first, far_last = pieces[5 * own : 5 * own + 5]
        for n, z in enumerate((z_lo, 1 - z_lo)):
            put(which, here.at[n], z, x_at, 0, BLOCK)
            put(which, from_left.at[n], z, left, 0, BLOCK)
            put(which, from_right.at[n], z, right, 0, BLOCK)
            put(which, far_first.at[n], z, far, 0, CUT)
            put(which, far_last.at[n], z, far, CUT, BLOCK - CUT)

    def whole(which):
        pltpu.make_async_copy(w.at[which], w.at[which], sems.at[which]).wait()

    eye = identity(WIN)
    for at, size in column_chunks(D, WIN):
        v_t[at : at + size, :] = mm_nt(eye[:size, :size], values[:, at : at + size])
    whole(0)
    for at, size in column_chunks(D, CHUNK):
        for g in range(2):
            rows = x[g * 16 : g * 16 + 16].reshape(S, D)
            query[g * S : g * S + S, at : at + size] = mm(rows, w[0, :, at : at + size]).astype(BF16)
    valid = lax.broadcasted_iota(jnp.int32, (SLOTS, T), 0) < length
    for head in range(H):
        at = window(head)
        masked = keys[:, at : at + WIN] * lane_mask(head, at, WIN)
        scores = mm_nt(masked, query[:, at : at + WIN])
        expo, over[head] = softmax_cols(jnp.where(valid, scores, -1e30))
        weights[head] = expo.astype(BF16)
    for head in range(H):
        mine = slice(head * HEAD, head * HEAD + HEAD)
        ctx_t[mine, :] = mm(v_t[mine, :].astype(BF16), weights[head]) * over[head]
    for g in range(2):
        rows = slice(g * S, g * S + S)
        ctx[rows, :] = mm_nt(eye, ctx_t[:, rows].astype(BF16)).astype(BF16)
    whole(1)
    for at, size in column_chunks(D, WIN):
        cols = slice(at, at + size)
        for g in range(2):
            value = x[g * 16 : g * 16 + 16, :, cols].astype(F32).reshape(S, size)
            value = value + mm(ctx[g * S : g * S + S, :], w[1, :, cols])
            value = value.reshape(16, 2, 8, size)
            for f in range(2):
                out[f, g * 128 : g * 128 + 128, cols] = value[:, f].reshape(128, size).astype(BF16)


def vmem(*shape):
    return pltpu.VMEM(shape, BF16)


def call(kernel, name, shape, scratch, flops, transcendentals, *args, smem=0, anywhere=0):
    spaces = [pltpu.SMEM] * smem + [pltpu.VMEM] * (len(args) - smem - anywhere) + [pl.ANY] * anywhere
    return pl.pallas_call(
        kernel,
        out_shape=jax.ShapeDtypeStruct(shape, BF16),
        in_specs=[pl.BlockSpec(memory_space=space) for space in spaces],
        out_specs=pl.BlockSpec(memory_space=pltpu.VMEM),
        scratch_shapes=scratch,
        compiler_params=pltpu.CompilerParams(vmem_limit_bytes=22 * 1024 * 1024),
        cost_estimate=pl.CostEstimate(
            flops=flops, bytes_accessed=13_000_000, transcendentals=transcendentals
        ),
        name=name,
    )(*args)


def spatial(*args):
    scratch = [vmem(T, D), vmem(T, 3 * D), vmem(H, S, S), vmem(T, D)]
    return call(spatial_kernel, "spatial", (32, 16, D), scratch, 8_000_000_000, 2_100_000, *args)


def temporal(*args):
    scratch = [
        vmem(T, D),
        vmem(T, 3 * D),
        vmem(H, S, S),
        vmem(T, D),
        vmem(T, D),
        pltpu.VMEM((H, 1, S), F32),
        pltpu.VMEM((D, S), F32),
        pltpu.VMEM((D, S), F32),
        pltpu.VMEM((LANES, T, 128), F32),
    ]
    return call(temporal_kernel, "temporal", (32, 16, D), scratch, 8_000_000_000, 600_000, *args)


def cross(place, x, keys, values, pieces):
    scratch = [
        vmem(2, D, D),
        vmem(T, D),
        vmem(H, SLOTS, T),
        pltpu.VMEM((H, 1, T), F32),
        pltpu.VMEM((D, SLOTS), F32),
        pltpu.VMEM((D, T), F32),
        vmem(T, D),
        pltpu.SemaphoreType.DMA((2,)),
    ]
    args = (place, x, keys, values, *pieces)
    return call(
        cross_kernel, "cross", (2, S, D), scratch, 4_000_000_000, 1_000_000, *args, smem=1, anywhere=10
    )


def shift(array, axis, by, size):
    return lax.ppermute(array, axis, [(i, (i + by) % size) for i in range(size)])


def gather_y(cross_query, cross_out):
    mine = jnp.where(lax.axis_index("core") == 0, cross_query, cross_out)
    return [shift(mine, "y", by, 4) for by in (3, 2, 1)] + [mine]


def in_order(rows):
    found = jnp.stack(rows + rows[:3])
    ordered = lax.dynamic_slice_in_dim(found, 3 - lax.axis_index("y"), 4, axis=0)
    return ordered.reshape(BLOCK, D)


def over_core(piece):
    return shift(piece, "core", 1, 2)


def body(
    latent,
    modulation,
    w_spatial_qkv,
    w_spatial_out,
    w_temporal_qkv,
    w_temporal_out,
    cross_query,
    cross_out,
    text_keys,
    text_values,
    text_len,
):
    rows = gather_y(cross_query, cross_out)
    after_spatial = spatial(latent.reshape(T, D), modulation, w_spatial_qkv, w_spatial_out)
    rows, after_spatial = lax.optimization_barrier((rows, after_spatial))
    placed = lax.all_to_all(after_spatial, SEQ, split_axis=0, concat_axis=0, tiled=True)
    block = in_order(rows)
    here = jnp.stack([block, shift(block, "z_lo", 1, 2)])
    left = shift(here, "x", 1, 4)
    right = shift(here, "x", -1, 4)
    after_temporal = temporal(placed, modulation, w_temporal_qkv, w_temporal_out)
    returned = lax.all_to_all(after_temporal, SEQ, split_axis=0, concat_axis=0, tiled=True)
    far_first = shift(left[:, :CUT], "x", 1, 4)
    far_last = shift(right[:, CUT:], "x", -1, 4)
    pieces = [here, left, right, far_first, far_last]
    pieces = pieces + [over_core(piece) for piece in pieces]
    place = jnp.stack(
        [text_len[0], lax.axis_index("core"), lax.axis_index("z_lo"), lax.axis_index("x")]
    ).astype(jnp.int32)
    fill = ((0, SLOTS - text_keys.shape[0]), (0, 0))
    keys, values = jnp.pad(text_keys, fill), jnp.pad(text_values, fill)
    return cross(place, returned, keys, values, pieces)


def solution(mesh):
    fine = Mesh(mesh.devices.reshape(2, 4, 4, 2, 2), ("z_lo", "x", "y", "z_hi", "core"))
    part = ("z_hi", "core")
    placed = (
        P(ALL, None, None),
        P(part, None),
        P(),
        P(),
        P(),
        P(),
        P(SEQ, None),
        P(SEQ, None),
        P(part, None),
        P(part, None),
        P(part),
    )
    return jax.shard_map(
        body, mesh=fine, in_specs=placed, out_specs=P(ALL, None, None), check_vma=False
    )
```

```python
import jax
import jax.numpy as jnp
import numpy as np
from jax import lax
from jax.experimental import pallas as pl
from jax.experimental.pallas import tpu as pltpu
from jax.sharding import Mesh, PartitionSpec as P

H = 16
HEAD = 72
LANES = 9
D = 1152
S = 256
T = 512
WIN = 256
SLOTS = 128
BLOCK = 144
CHUNK = 512
EXP_SCALE = float(np.log2(np.e) / np.sqrt(72.0))
F32 = jnp.float32
BF16 = jnp.bfloat16
NT = (((1,), (1,)), ((), ()))
SEQ = ("z_lo", "x", "y")
ALL = ("z_hi", "core", "z_lo", "x", "y")


def mm(a, b):
    return jnp.dot(a, b, preferred_element_type=F32)


def mm_nt(a, b):
    return lax.dot_general(a, b, NT, preferred_element_type=F32)


def window(head):
    return min(HEAD * head // 128 * 128, D - WIN)


def lane_mask(head, at, size):
    lane = lax.broadcasted_iota(jnp.int32, (1, size), 1) + at
    inside = (lane >= HEAD * head) & (lane < HEAD * head + HEAD)
    return jnp.where(inside, 1.0, 0.0).astype(BF16)


def heads_of(at, size):
    return [h for h in range(H) if h * HEAD < at + size and h * HEAD + HEAD > at]


def identity(n):
    rows = lax.broadcasted_iota(jnp.int32, (n, n), 0)
    cols = lax.broadcasted_iota(jnp.int32, (n, n), 1)
    return jnp.where(rows == cols, 1.0, 0.0).astype(BF16)


def norm_mod(values, shift, scale):
    mean = jnp.mean(values, axis=-1, keepdims=True)
    centered = values - mean
    var = jnp.mean(centered * centered, axis=-1, keepdims=True)
    return (centered * lax.rsqrt(var + 1e-06) * (1.0 + scale) + shift).astype(BF16)


def column_chunks(width, chunk):
    return [(at, min(chunk, width - at)) for at in range(0, width, chunk)]


def halves(body):
    def step(g, carry):
        body(g, pl.ds(pl.multiple_of(g * S, S), S))
        return carry

    lax.fori_loop(0, 2, step, 0)


def fetch(src, dst, sems):
    copies = []
    for n, (at, size) in enumerate(column_chunks(src.shape[1], CHUNK)):
        cols = pl.ds(at, size)
        copies.append(pltpu.make_async_copy(src.at[:, cols], dst.at[:, cols], sems.at[n]))
        copies[-1].start()
    return copies


def project_qkv(xn, w, copies, qkv):
    for copy, (at, size) in zip(copies, column_chunks(3 * D, CHUNK)):
        copy.wait()
        for rows in (slice(0, S), slice(S, T)):
            qkv[rows, at : at + size] = mm(xn[rows, :], w[:, at : at + size]).astype(BF16)


def softmax_rows(scores):
    top = jnp.max(scores, axis=1, keepdims=True)
    expo = jnp.exp2(scores * EXP_SCALE - top * EXP_SCALE)
    return (expo * (1.0 / jnp.sum(expo, axis=1, keepdims=True))).astype(BF16)


def softmax_cols(scores):
    top = jnp.max(scores, axis=0, keepdims=True)
    expo = jnp.exp2(scores * EXP_SCALE - top * EXP_SCALE)
    return expo, 1.0 / jnp.sum(expo, axis=0, keepdims=True)


def softmax_blocks(scores):
    low = lax.broadcasted_iota(jnp.int32, (64, 128), 1) < 64
    left, over_left = softmax_cols(jnp.where(low, scores[0:64, :128], scores[64:128, :128]))
    right, over_right = softmax_cols(jnp.where(low, scores[128:192, 128:], scores[192:256, 128:]))
    zero = jnp.zeros((64, 128), F32)
    wide = jnp.concatenate(
        [
            jnp.concatenate([jnp.where(low, left, zero), zero], 1),
            jnp.concatenate([jnp.where(low, zero, left), zero], 1),
            jnp.concatenate([zero, jnp.where(low, right, zero)], 1),
            jnp.concatenate([zero, jnp.where(low, zero, right)], 1),
        ],
        0,
    )
    return wide.astype(BF16), jnp.concatenate([over_left, over_right], 1)


def spatial_kernel(lat, mod, w_hbm, wo_hbm, out, xn, qkv, weights, ctx, w, wo, sem, wsems):
    copies = fetch(w_hbm, w, wsems)
    last = pltpu.make_async_copy(wo_hbm, wo, sem)
    last.start()
    shift, scale, gate = mod[0:1, :], mod[1:2, :], mod[2:3, :]

    def norm_rows(i, carry):
        rows = pl.ds(pl.multiple_of(i * 64, 64), 64)
        xn[rows, :] = norm_mod(lat[rows, :].astype(F32), shift, scale)
        return carry

    lax.fori_loop(0, T // 64, norm_rows, 0, unroll=2)
    project_qkv(xn, w, copies, qkv)

    def attend(g, rows):
        for head in range(H):
            at = window(head)
            query = qkv[rows, at : at + WIN] * lane_mask(head, at, WIN)
            weights[head] = softmax_rows(mm_nt(query, qkv[rows, D + at : D + at + WIN]))
        for at, size in column_chunks(D, WIN):
            values = qkv[rows, 2 * D + at : 2 * D + at + size]
            mixed = 0
            for head in heads_of(at, size):
                mixed = mixed + mm(weights[head], values * lane_mask(head, at, size))
            ctx[rows, at : at + size] = mixed.astype(BF16)

    halves(attend)
    last.wait()
    for at, size in column_chunks(D, WIN):
        cols = slice(at, at + size)
        parts = []
        for rows in (slice(0, S), slice(S, T)):
            value = lat[rows, cols].astype(F32) + gate[:, cols] * mm(ctx[rows, :], wo[:, cols])
            parts.append(value.reshape(32, 8, size))
        out[:, :, cols] = jnp.concatenate(parts, axis=1).astype(BF16)


def temporal_kernel(
    x, mod, w_hbm, wo_hbm, out, xn, qkv, weights, ctx, rest, over, v_t, ctx_t, wide, w, wo, sem, wsems
):
    copies = fetch(w_hbm, w, wsems)
    last = pltpu.make_async_copy(wo_hbm, wo, sem)
    last.start()
    shift, scale, gate = mod[3:4, :], mod[4:5, :], mod[5:6, :]

    def widen(i, carry):
        value = x[i].astype(F32)
        for j in range(LANES):
            wide[j, pl.ds(pl.multiple_of(i * 16, 16), 16), :] = value[:, j * 128 : j * 128 + 128]
        return carry

    lax.fori_loop(0, 32, widen, 0, unroll=4)

    def norm_rows(p, carry):
        picked = pl.ds(p, 64, stride=8)
        values = jnp.concatenate([wide[j, picked, :] for j in range(LANES)], axis=1)
        rows = pl.ds(pl.multiple_of(p * 64, 64), 64)
        rest[rows, :] = values.astype(BF16)
        xn[rows, :] = norm_mod(values, shift, scale)
        return carry

    lax.fori_loop(0, 8, norm_rows, 0, unroll=2)
    project_qkv(xn, w, copies, qkv)
    eye = identity(WIN)

    def attend(g, rows):
        for at, size in column_chunks(D, WIN):
            v_t[at : at + size, :] = mm_nt(eye[:size, :size], qkv[rows, 2 * D + at : 2 * D + at + size])
        for head in range(H):
            at = window(head)
            query = qkv[rows, at : at + WIN] * lane_mask(head, at, WIN)
            weights[head], over[head] = softmax_blocks(mm_nt(qkv[rows, D + at : D + at + WIN], query))
        for head in range(H):
            mine = slice(head * HEAD, head * HEAD + HEAD)
            ctx_t[mine, :] = mm(v_t[mine, :].astype(BF16), weights[head]) * over[head]
        ctx[rows, :] = mm_nt(eye, ctx_t[...].astype(BF16)).astype(BF16)

    halves(attend)
    last.wait()
    for at, size in column_chunks(D, WIN):
        cols = slice(at, at + size)
        for g in range(2):
            rows = slice(g * S, g * S + S)
            value = rest[rows, cols].astype(F32) + gate[:, cols] * mm(ctx[rows, :], wo[:, cols])
            for p in range(4):
                for j in range(size // 128):
                    piece = value[p * 64 : p * 64 + 64, j * 128 : j * 128 + 128]
                    wide[at // 128 + j, pl.ds(g * 4 + p, 64, stride=8), :] = piece

    def narrow(i, carry):
        rows = pl.ds(pl.multiple_of(i * 16, 16), 16)
        out[i] = jnp.concatenate([wide[j, rows, :] for j in range(LANES)], axis=1).astype(BF16)
        return carry

    lax.fori_loop(0, 32, narrow, 0, unroll=4)


def cross_kernel(place, x, keys, values, *refs):
    pieces, (out, w, query, weights, over, v_t, ctx_t, ctx, sems) = refs[:10], refs[10:]
    length, core, z_lo, x_at = place[0], place[1], place[2], place[3]

    def put(which, src, z, x_from):
        row = pl.multiple_of(z * (D // 2) + x_from * BLOCK, 16)
        pltpu.make_async_copy(src, w.at[which, pl.ds(row, BLOCK), :], sems.at[which]).start()

    left, right, far = (x_at + 3) % 4, (x_at + 1) % 4, (x_at + 2) % 4
    for own in range(2):
        which = core if own == 0 else 1 - core
        here, from_left, from_right, far_same, far_other = pieces[5 * own : 5 * own + 5]
        for n, z in enumerate((z_lo, 1 - z_lo)):
            put(which, here.at[n], z, x_at)
            put(which, from_left.at[n], z, left)
            put(which, from_right.at[n], z, right)
        put(which, far_same, z_lo, far)
        put(which, far_other, 1 - z_lo, far)

    def whole(which):
        pltpu.make_async_copy(w.at[which], w.at[which], sems.at[which]).wait()

    eye = identity(WIN)
    for at, size in column_chunks(D, WIN):
        v_t[at : at + size, :] = mm_nt(eye[:size, :size], values[:, at : at + size])
    whole(0)
    for at, size in column_chunks(D, CHUNK):
        for g in range(2):
            rows = x[g * 16 : g * 16 + 16].reshape(S, D)
            query[g * S : g * S + S, at : at + size] = mm(rows, w[0, :, at : at + size]).astype(BF16)
    valid = lax.broadcasted_iota(jnp.int32, (SLOTS, T), 0) < length
    for head in range(H):
        at = window(head)
        masked = keys[:, at : at + WIN] * lane_mask(head, at, WIN)
        scores = mm_nt(masked, query[:, at : at + WIN])
        expo, over[head] = softmax_cols(jnp.where(valid, scores, -1e30))
        weights[head] = expo.astype(BF16)
    for head in range(H):
        mine = slice(head * HEAD, head * HEAD + HEAD)
        ctx_t[mine, :] = mm(v_t[mine, :].astype(BF16), weights[head]) * over[head]
    for g in range(2):
        rows = slice(g * S, g * S + S)
        ctx[rows, :] = mm_nt(eye, ctx_t[:, rows].astype(BF16)).astype(BF16)
    whole(1)
    for at, size in column_chunks(D, WIN):
        cols = slice(at, at + size)
        for g in range(2):
            value = x[g * 16 : g * 16 + 16, :, cols].astype(F32).reshape(S, size)
            value = value + mm(ctx[g * S : g * S + S, :], w[1, :, cols])
            value = value.reshape(16, 2, 8, size)
            for f in range(2):
                out[f, g * 128 : g * 128 + 128, cols] = value[:, f].reshape(128, size).astype(BF16)


def vmem(*shape):
    return pltpu.VMEM(shape, BF16)


def weight_scratch():
    n = len(column_chunks(3 * D, CHUNK))
    return [
        vmem(D, 3 * D),
        vmem(D, D),
        pltpu.SemaphoreType.DMA,
        pltpu.SemaphoreType.DMA((n,)),
    ]


def call(kernel, name, shape, scratch, flops, transcendentals, spaces, *args):
    args = [
        pltpu.with_memory_space_constraint(arg, space) if space == pltpu.HBM else arg
        for arg, space in zip(args, spaces)
    ]
    return pl.pallas_call(
        kernel,
        out_shape=jax.ShapeDtypeStruct(shape, BF16),
        in_specs=[pl.BlockSpec(memory_space=pl.ANY if space == pltpu.HBM else space) for space in spaces],
        out_specs=pl.BlockSpec(memory_space=pltpu.VMEM),
        scratch_shapes=scratch,
        compiler_params=pltpu.CompilerParams(vmem_limit_bytes=34 * 1024 * 1024),
        cost_estimate=pl.CostEstimate(
            flops=flops, bytes_accessed=13_000_000, transcendentals=transcendentals
        ),
        name=name,
    )(*args)


def spatial(*args):
    scratch = [vmem(T, D), vmem(T, 3 * D), vmem(H, S, S), vmem(T, D)]
    scratch = scratch + weight_scratch()
    spaces = [pltpu.VMEM, pltpu.VMEM, pltpu.HBM, pltpu.HBM]
    return call(spatial_kernel, "spatial", (32, 16, D), scratch, 8_000_000_000, 2_100_000, spaces, *args)


def temporal(*args):
    scratch = [
        vmem(T, D),
        vmem(T, 3 * D),
        vmem(H, S, S),
        vmem(T, D),
        vmem(T, D),
        pltpu.VMEM((H, 1, S), F32),
        pltpu.VMEM((D, S), F32),
        pltpu.VMEM((D, S), F32),
        pltpu.VMEM((LANES, T, 128), F32),
    ]
    scratch = scratch + weight_scratch()
    spaces = [pltpu.VMEM, pltpu.VMEM, pltpu.HBM, pltpu.HBM]
    return call(temporal_kernel, "temporal", (32, 16, D), scratch, 8_000_000_000, 600_000, spaces, *args)


def cross(place, x, keys, values, pieces):
    scratch = [
        vmem(2, D, D),
        vmem(T, D),
        vmem(H, SLOTS, T),
        pltpu.VMEM((H, 1, T), F32),
        pltpu.VMEM((D, SLOTS), F32),
        pltpu.VMEM((D, T), F32),
        vmem(T, D),
        pltpu.SemaphoreType.DMA((2,)),
    ]
    args = (place, x, keys, values, *pieces)
    spaces = [pltpu.SMEM] + [pltpu.VMEM] * 3 + [pl.ANY] * len(pieces)
    return call(cross_kernel, "cross", (2, S, D), scratch, 4_000_000_000, 1_000_000, spaces, *args)


def shift(array, axis, by, size):
    return lax.ppermute(array, axis, [(i, (i + by) % size) for i in range(size)])


def over_y(rows):
    return [shift(rows, "y", by, 4) for by in (3, 2, 1)] + [rows]


def in_order(rows):
    found = jnp.stack(rows + rows[:3])
    ordered = lax.dynamic_slice_in_dim(found, 3 - lax.axis_index("y"), 4, axis=0)
    return ordered.reshape(BLOCK, D)


def over_core(piece):
    return shift(piece, "core", 1, 2)


def body(
    latent,
    modulation,
    w_spatial_qkv,
    w_spatial_out,
    w_temporal_qkv,
    w_temporal_out,
    cross_query,
    cross_out,
    text_keys,
    text_values,
    text_len,
):
    mine = jnp.where(lax.axis_index("core") == 0, cross_query, cross_out)
    rows = over_y(mine)
    far_mine = shift(mine, "x", 2, 4)
    after_spatial = spatial(latent.reshape(T, D), modulation, w_spatial_qkv, w_spatial_out)
    rows, far_mine, after_spatial = lax.optimization_barrier((rows, far_mine, after_spatial))
    placed = lax.all_to_all(after_spatial, SEQ, split_axis=0, concat_axis=0, tiled=True)
    block = in_order(rows)
    far_rows = over_y(far_mine)
    here = jnp.stack([block, shift(block, "z_lo", 1, 2)])
    far_same = in_order(far_rows)
    here, far_same, placed = lax.optimization_barrier((here, far_same, placed))
    left = shift(here, "x", 1, 4)
    right = shift(here, "x", -1, 4)
    far_other = shift(far_same, "z_lo", 1, 2)
    after_temporal = temporal(placed, modulation, w_temporal_qkv, w_temporal_out)
    pieces = [here, left, right, far_same, far_other]
    pieces, after_temporal = lax.optimization_barrier((pieces, after_temporal))
    returned = lax.all_to_all(after_temporal, SEQ, split_axis=0, concat_axis=0, tiled=True)
    pieces = pieces + [over_core(piece) for piece in pieces]
    place = jnp.stack(
        [text_len[0], lax.axis_index("core"), lax.axis_index("z_lo"), lax.axis_index("x")]
    ).astype(jnp.int32)
    fill = ((0, SLOTS - text_keys.shape[0]), (0, 0))
    keys, values = jnp.pad(text_keys, fill), jnp.pad(text_values, fill)
    return cross(place, returned, keys, values, pieces)


def solution(mesh):
    fine = Mesh(mesh.devices.reshape(2, 4, 4, 2, 2), ("z_lo", "x", "y", "z_hi", "core"))
    part = ("z_hi", "core")
    placed = (
        P(ALL, None, None),
        P(part, None),
        P(),
        P(),
        P(),
        P(),
        P(SEQ, None),
        P(SEQ, None),
        P(part, None),
        P(part, None),
        P(part),
    )
    return jax.shard_map(
        body, mesh=fine, in_specs=placed, out_specs=P(ALL, None, None), check_vma=False
    )
```

```python
import jax
import jax.numpy as jnp
import numpy as np
from jax import lax
from jax.experimental import pallas as pl
from jax.experimental.pallas import tpu as pltpu
from jax.sharding import Mesh, PartitionSpec as P

H = 16
HEAD = 72
LANES = 9
D = 1152
S = 256
T = 512
WIN = 256
SLOTS = 128
BLOCK = 144
CHUNK = 512
EXP_SCALE = float(np.log2(np.e) / np.sqrt(72.0))
F32 = jnp.float32
BF16 = jnp.bfloat16
NT = (((1,), (1,)), ((), ()))
SEQ = ("z_lo", "x_hi", "x_lo", "y")
ALL = ("z_hi", "core") + SEQ


def mm(a, b):
    return jnp.dot(a, b, preferred_element_type=F32)


def mm_nt(a, b):
    return lax.dot_general(a, b, NT, preferred_element_type=F32)


def window(head):
    return min(HEAD * head // 128 * 128, D - WIN)


def lane_mask(head, at, size):
    lane = lax.broadcasted_iota(jnp.int32, (1, size), 1) + at
    inside = (lane >= HEAD * head) & (lane < HEAD * head + HEAD)
    return jnp.where(inside, 1.0, 0.0).astype(BF16)


def heads_of(at, size):
    return [h for h in range(H) if h * HEAD < at + size and h * HEAD + HEAD > at]


def identity(n):
    rows = lax.broadcasted_iota(jnp.int32, (n, n), 0)
    cols = lax.broadcasted_iota(jnp.int32, (n, n), 1)
    return jnp.where(rows == cols, 1.0, 0.0).astype(BF16)


def norm_mod(values, shift, scale):
    mean = jnp.mean(values, axis=-1, keepdims=True)
    centered = values - mean
    var = jnp.mean(centered * centered, axis=-1, keepdims=True)
    return (centered * lax.rsqrt(var + 1e-06) * (1.0 + scale) + shift).astype(BF16)


def column_chunks(width, chunk):
    return [(at, min(chunk, width - at)) for at in range(0, width, chunk)]


def halves(body):
    def step(g, carry):
        body(g, pl.ds(pl.multiple_of(g * S, S), S))
        return carry

    lax.fori_loop(0, 2, step, 0)


def fetch(src, dst, sems):
    copies = []
    for n, (at, size) in enumerate(column_chunks(src.shape[1], CHUNK)):
        cols = pl.ds(at, size)
        copies.append(pltpu.make_async_copy(src.at[:, cols], dst.at[:, cols], sems.at[n]))
        copies[-1].start()
    return copies


def project_qkv(xn, w, copies, qkv):
    for copy, (at, size) in zip(copies, column_chunks(3 * D, CHUNK)):
        copy.wait()
        for rows in (slice(0, S), slice(S, T)):
            qkv[rows, at : at + size] = mm(xn[rows, :], w[:, at : at + size]).astype(BF16)


def softmax_rows(scores):
    top = jnp.max(scores, axis=1, keepdims=True)
    expo = jnp.exp2(scores * EXP_SCALE - top * EXP_SCALE)
    return (expo * (1.0 / jnp.sum(expo, axis=1, keepdims=True))).astype(BF16)


def softmax_cols(scores):
    top = jnp.max(scores, axis=0, keepdims=True)
    expo = jnp.exp2(scores * EXP_SCALE - top * EXP_SCALE)
    return expo, 1.0 / jnp.sum(expo, axis=0, keepdims=True)


def softmax_blocks(scores):
    low = lax.broadcasted_iota(jnp.int32, (64, 128), 1) < 64
    left, over_left = softmax_cols(jnp.where(low, scores[0:64, :128], scores[64:128, :128]))
    right, over_right = softmax_cols(jnp.where(low, scores[128:192, 128:], scores[192:256, 128:]))
    zero = jnp.zeros((64, 128), F32)
    wide = jnp.concatenate(
        [
            jnp.concatenate([jnp.where(low, left, zero), zero], 1),
            jnp.concatenate([jnp.where(low, zero, left), zero], 1),
            jnp.concatenate([zero, jnp.where(low, right, zero)], 1),
            jnp.concatenate([zero, jnp.where(low, zero, right)], 1),
        ],
        0,
    )
    return wide.astype(BF16), jnp.concatenate([over_left, over_right], 1)


def spatial_kernel(lat, mod, w_hbm, wo_hbm, out, xn, qkv, weights, ctx, w, wo, sem, wsems):
    copies = fetch(w_hbm, w, wsems)
    last = pltpu.make_async_copy(wo_hbm, wo, sem)
    last.start()
    shift, scale, gate = mod[0:1, :], mod[1:2, :], mod[2:3, :]

    def norm_rows(i, carry):
        rows = pl.ds(pl.multiple_of(i * 64, 64), 64)
        xn[rows, :] = norm_mod(lat[rows, :].astype(F32), shift, scale)
        return carry

    lax.fori_loop(0, T // 64, norm_rows, 0, unroll=2)
    project_qkv(xn, w, copies, qkv)

    def attend(g, rows):
        for head in range(H):
            at = window(head)
            query = qkv[rows, at : at + WIN] * lane_mask(head, at, WIN)
            weights[head] = softmax_rows(mm_nt(query, qkv[rows, D + at : D + at + WIN]))
        for at, size in column_chunks(D, WIN):
            values = qkv[rows, 2 * D + at : 2 * D + at + size]
            mixed = 0
            for head in heads_of(at, size):
                mixed = mixed + mm(weights[head], values * lane_mask(head, at, size))
            ctx[rows, at : at + size] = mixed.astype(BF16)

    halves(attend)
    last.wait()
    for at, size in column_chunks(D, WIN):
        cols = slice(at, at + size)
        parts = []
        for rows in (slice(0, S), slice(S, T)):
            value = lat[rows, cols].astype(F32) + gate[:, cols] * mm(ctx[rows, :], wo[:, cols])
            parts.append(value.reshape(32, 8, size))
        out[:, :, cols] = jnp.concatenate(parts, axis=1).astype(BF16)


def temporal_kernel(
    x, mod, w_hbm, wo_hbm, out, xn, qkv, weights, ctx, rest, over, v_t, ctx_t, wide, w, wo, sem, wsems
):
    copies = fetch(w_hbm, w, wsems)
    last = pltpu.make_async_copy(wo_hbm, wo, sem)
    last.start()
    shift, scale, gate = mod[3:4, :], mod[4:5, :], mod[5:6, :]

    def widen(i, carry):
        value = x[i].astype(F32)
        for j in range(LANES):
            wide[j, pl.ds(pl.multiple_of(i * 16, 16), 16), :] = value[:, j * 128 : j * 128 + 128]
        return carry

    lax.fori_loop(0, 32, widen, 0, unroll=4)

    def norm_rows(p, carry):
        picked = pl.ds(p, 64, stride=8)
        values = jnp.concatenate([wide[j, picked, :] for j in range(LANES)], axis=1)
        rows = pl.ds(pl.multiple_of(p * 64, 64), 64)
        rest[rows, :] = values.astype(BF16)
        xn[rows, :] = norm_mod(values, shift, scale)
        return carry

    lax.fori_loop(0, 8, norm_rows, 0, unroll=2)
    project_qkv(xn, w, copies, qkv)
    eye = identity(WIN)

    def attend(g, rows):
        for at, size in column_chunks(D, WIN):
            v_t[at : at + size, :] = mm_nt(eye[:size, :size], qkv[rows, 2 * D + at : 2 * D + at + size])
        for head in range(H):
            at = window(head)
            query = qkv[rows, at : at + WIN] * lane_mask(head, at, WIN)
            weights[head], over[head] = softmax_blocks(mm_nt(qkv[rows, D + at : D + at + WIN], query))
        for head in range(H):
            mine = slice(head * HEAD, head * HEAD + HEAD)
            ctx_t[mine, :] = mm(v_t[mine, :].astype(BF16), weights[head]) * over[head]
        ctx[rows, :] = mm_nt(eye, ctx_t[...].astype(BF16)).astype(BF16)

    halves(attend)
    last.wait()
    for at, size in column_chunks(D, WIN):
        cols = slice(at, at + size)
        for g in range(2):
            rows = slice(g * S, g * S + S)
            value = rest[rows, cols].astype(F32) + gate[:, cols] * mm(ctx[rows, :], wo[:, cols])
            for p in range(4):
                for j in range(size // 128):
                    piece = value[p * 64 : p * 64 + 64, j * 128 : j * 128 + 128]
                    wide[at // 128 + j, pl.ds(g * 4 + p, 64, stride=8), :] = piece

    def narrow(i, carry):
        rows = pl.ds(pl.multiple_of(i * 16, 16), 16)
        out[i] = jnp.concatenate([wide[j, rows, :] for j in range(LANES)], axis=1).astype(BF16)
        return carry

    lax.fori_loop(0, 32, narrow, 0, unroll=4)


def cross_kernel(place, x, keys, values, *refs):
    pieces, (out, w, query, weights, over, v_t, ctx_t, ctx, sems) = refs[:6], refs[6:]
    length, core, x_lo = place[0], place[1], place[2]

    def put(which, src, z, x):
        row = pl.multiple_of(z * (D // 2) + x * BLOCK, 16)
        pltpu.make_async_copy(src, w.at[which, pl.ds(row, BLOCK), :], sems.at[which]).start()

    for own in range(2):
        which = core if own == 0 else 1 - core
        same, other_first, other_last = pieces[3 * own : 3 * own + 3]
        for z in range(2):
            put(which, same.at[0, z], z, x_lo)
            put(which, same.at[1, z], z, 2 + x_lo)
            put(which, other_first.at[z], z, 1 - x_lo)
            put(which, other_last.at[z], z, 3 - x_lo)

    def whole(which):
        pltpu.make_async_copy(w.at[which], w.at[which], sems.at[which]).wait()

    eye = identity(WIN)
    for at, size in column_chunks(D, WIN):
        v_t[at : at + size, :] = mm_nt(eye[:size, :size], values[:, at : at + size])
    whole(0)
    for at, size in column_chunks(D, CHUNK):
        for g in range(2):
            rows = x[g * 16 : g * 16 + 16].reshape(S, D)
            query[g * S : g * S + S, at : at + size] = mm(rows, w[0, :, at : at + size]).astype(BF16)
    valid = lax.broadcasted_iota(jnp.int32, (SLOTS, T), 0) < length
    for head in range(H):
        at = window(head)
        masked = keys[:, at : at + WIN] * lane_mask(head, at, WIN)
        scores = mm_nt(masked, query[:, at : at + WIN])
        expo, over[head] = softmax_cols(jnp.where(valid, scores, -1e30))
        weights[head] = expo.astype(BF16)
    for head in range(H):
        mine = slice(head * HEAD, head * HEAD + HEAD)
        ctx_t[mine, :] = mm(v_t[mine, :].astype(BF16), weights[head]) * over[head]
    for g in range(2):
        rows = slice(g * S, g * S + S)
        ctx[rows, :] = mm_nt(eye, ctx_t[:, rows].astype(BF16)).astype(BF16)
    whole(1)
    for at, size in column_chunks(D, WIN):
        cols = slice(at, at + size)
        for g in range(2):
            value = x[g * 16 : g * 16 + 16, :, cols].astype(F32).reshape(S, size)
            value = value + mm(ctx[g * S : g * S + S, :], w[1, :, cols])
            value = value.reshape(16, 2, 8, size)
            for f in range(2):
                out[f, g * 128 : g * 128 + 128, cols] = value[:, f].reshape(128, size).astype(BF16)


def vmem(*shape):
    return pltpu.VMEM(shape, BF16)


def weight_scratch():
    n = len(column_chunks(3 * D, CHUNK))
    return [
        vmem(D, 3 * D),
        vmem(D, D),
        pltpu.SemaphoreType.DMA,
        pltpu.SemaphoreType.DMA((n,)),
    ]


def call(kernel, name, shape, scratch, flops, transcendentals, spaces, *args):
    args = [
        pltpu.with_memory_space_constraint(arg, space) if space == pltpu.HBM else arg
        for arg, space in zip(args, spaces)
    ]
    return pl.pallas_call(
        kernel,
        out_shape=jax.ShapeDtypeStruct(shape, BF16),
        in_specs=[pl.BlockSpec(memory_space=pl.ANY if space == pltpu.HBM else space) for space in spaces],
        out_specs=pl.BlockSpec(memory_space=pltpu.VMEM),
        scratch_shapes=scratch,
        compiler_params=pltpu.CompilerParams(vmem_limit_bytes=34 * 1024 * 1024),
        cost_estimate=pl.CostEstimate(
            flops=flops, bytes_accessed=13_000_000, transcendentals=transcendentals
        ),
        name=name,
    )(*args)


def spatial(*args):
    scratch = [vmem(T, D), vmem(T, 3 * D), vmem(H, S, S), vmem(T, D)]
    scratch = scratch + weight_scratch()
    spaces = [pltpu.VMEM, pltpu.VMEM, pltpu.HBM, pltpu.HBM]
    return call(spatial_kernel, "spatial", (32, 16, D), scratch, 8_000_000_000, 2_100_000, spaces, *args)


def temporal(*args):
    scratch = [
        vmem(T, D),
        vmem(T, 3 * D),
        vmem(H, S, S),
        vmem(T, D),
        vmem(T, D),
        pltpu.VMEM((H, 1, S), F32),
        pltpu.VMEM((D, S), F32),
        pltpu.VMEM((D, S), F32),
        pltpu.VMEM((LANES, T, 128), F32),
    ]
    scratch = scratch + weight_scratch()
    spaces = [pltpu.VMEM, pltpu.VMEM, pltpu.HBM, pltpu.HBM]
    return call(temporal_kernel, "temporal", (32, 16, D), scratch, 8_000_000_000, 600_000, spaces, *args)


def cross(place, x, keys, values, pieces):
    scratch = [
        vmem(2, D, D),
        vmem(T, D),
        vmem(H, SLOTS, T),
        pltpu.VMEM((H, 1, T), F32),
        pltpu.VMEM((D, SLOTS), F32),
        pltpu.VMEM((D, T), F32),
        vmem(T, D),
        pltpu.SemaphoreType.DMA((2,)),
    ]
    args = (place, x, keys, values, *pieces)
    spaces = [pltpu.SMEM] + [pltpu.VMEM] * 3 + [pl.ANY] * len(pieces)
    return call(cross_kernel, "cross", (2, S, D), scratch, 4_000_000_000, 1_000_000, spaces, *args)


def shift(array, axes, by, size):
    return lax.ppermute(array, axes, [(i, (i + by) % size) for i in range(size)])


def gather_even(rows):
    copies = jnp.broadcast_to(rows[None], (16,) + rows.shape)
    axes = ("x_hi", "z_lo", "y")
    found = lax.all_to_all(copies, axes, split_axis=0, concat_axis=0, tiled=True)
    return found


def body(
    latent,
    modulation,
    w_spatial_qkv,
    w_spatial_out,
    w_temporal_qkv,
    w_temporal_out,
    cross_query,
    cross_out,
    text_keys,
    text_values,
    text_len,
):
    mine = jnp.where(lax.axis_index("core") == 0, cross_query, cross_out)
    found = gather_even(mine)
    after_spatial = spatial(latent.reshape(T, D), modulation, w_spatial_qkv, w_spatial_out)
    found, after_spatial = lax.optimization_barrier((found, after_spatial))
    placed = lax.all_to_all(after_spatial, SEQ, split_axis=0, concat_axis=0, tiled=True)
    same = found.reshape(2, 2, BLOCK, D)
    same, placed = lax.optimization_barrier((same, placed))
    other_first = shift(same[0], ("x_hi", "x_lo"), 1, 4)
    other_last = shift(same[1], ("x_hi", "x_lo"), -1, 4)
    after_temporal = temporal(placed, modulation, w_temporal_qkv, w_temporal_out)
    pieces = [same, other_first, other_last]
    pieces, after_temporal = lax.optimization_barrier((pieces, after_temporal))
    returned = lax.all_to_all(after_temporal, SEQ, split_axis=0, concat_axis=0, tiled=True)
    pieces = pieces + [shift(piece, "core", 1, 2) for piece in pieces]
    place = jnp.stack(
        [text_len[0], lax.axis_index("core"), lax.axis_index("x_lo")]
    ).astype(jnp.int32)
    fill = ((0, SLOTS - text_keys.shape[0]), (0, 0))
    keys, values = jnp.pad(text_keys, fill), jnp.pad(text_values, fill)
    return cross(place, returned, keys, values, pieces)


def solution(mesh):
    fine = Mesh(mesh.devices.reshape(2, 2, 2, 4, 2, 2), SEQ + ("z_hi", "core"))
    part = ("z_hi", "core")
    placed = (
        P(ALL, None, None),
        P(part, None),
        P(),
        P(),
        P(),
        P(),
        P(SEQ, None),
        P(SEQ, None),
        P(part, None),
        P(part, None),
        P(part),
    )
    return jax.shard_map(
        body, mesh=fine, in_specs=placed, out_specs=P(ALL, None, None), check_vma=False
    )
```

```python
import functools

import jax
import jax.numpy as jnp
import numpy as np
from jax import lax
from jax.experimental import pallas as pl
from jax.experimental.pallas import tpu as pltpu
from jax.sharding import Mesh, PartitionSpec as P

H = 16
HEAD = 72
LANES = 9
D = 1152
S = 256
T = 512
WIN = 256
SLOTS = 128
BLOCK = 144
CHUNK = 512
EXP_SCALE = float(np.log2(np.e) / np.sqrt(72.0))
F32 = jnp.float32
BF16 = jnp.bfloat16
NT = (((1,), (1,)), ((), ()))
SEQ = ("z_lo", "x_hi", "x_lo", "y")
ALL = ("z_hi", "core") + SEQ


def mm(a, b):
    return jnp.dot(a, b, preferred_element_type=F32)


def mm_nt(a, b):
    return lax.dot_general(a, b, NT, preferred_element_type=F32)


def window(head):
    return min(HEAD * head // 128 * 128, D - WIN)


def lane_mask(head, at, size):
    lane = lax.broadcasted_iota(jnp.int32, (1, size), 1) + at
    inside = (lane >= HEAD * head) & (lane < HEAD * head + HEAD)
    return jnp.where(inside, 1.0, 0.0).astype(BF16)


def heads_of(at, size):
    return [h for h in range(H) if h * HEAD < at + size and h * HEAD + HEAD > at]


def identity(n):
    rows = lax.broadcasted_iota(jnp.int32, (n, n), 0)
    cols = lax.broadcasted_iota(jnp.int32, (n, n), 1)
    return jnp.where(rows == cols, 1.0, 0.0).astype(BF16)


def norm_mod(values, shift, scale):
    mean = jnp.mean(values, axis=-1, keepdims=True)
    centered = values - mean
    var = jnp.mean(centered * centered, axis=-1, keepdims=True)
    return (centered * lax.rsqrt(var + 1e-06) * (1.0 + scale) + shift).astype(BF16)


def column_chunks(width, chunk):
    return [(at, min(chunk, width - at)) for at in range(0, width, chunk)]


def halves(body):
    def step(g, carry):
        body(g, pl.ds(pl.multiple_of(g * S, S), S))
        return carry

    lax.fori_loop(0, 2, step, 0)


def fetch(src, dst, sems):
    copies = []
    for n, (at, size) in enumerate(column_chunks(src.shape[1], CHUNK)):
        cols = pl.ds(at, size)
        copies.append(pltpu.make_async_copy(src.at[:, cols], dst.at[:, cols], sems.at[n]))
        copies[-1].start()
    return copies


def project_qkv(xn, w, copies, qkv):
    for copy, (at, size) in zip(copies, column_chunks(3 * D, CHUNK)):
        copy.wait()
        for lo in range(0, xn.shape[0], S):
            rows = slice(lo, lo + S)
            qkv[rows, at : at + size] = mm(xn[rows, :], w[:, at : at + size]).astype(BF16)


def softmax_rows(scores):
    top = jnp.max(scores, axis=1, keepdims=True)
    expo = jnp.exp2(scores * EXP_SCALE - top * EXP_SCALE)
    return (expo * (1.0 / jnp.sum(expo, axis=1, keepdims=True))).astype(BF16)


def softmax_cols(scores):
    top = jnp.max(scores, axis=0, keepdims=True)
    expo = jnp.exp2(scores * EXP_SCALE - top * EXP_SCALE)
    return expo, 1.0 / jnp.sum(expo, axis=0, keepdims=True)


def softmax_blocks(scores):
    low = lax.broadcasted_iota(jnp.int32, (64, 128), 1) < 64
    left, over_left = softmax_cols(jnp.where(low, scores[0:64, :128], scores[64:128, :128]))
    right, over_right = softmax_cols(jnp.where(low, scores[128:192, 128:], scores[192:256, 128:]))
    zero = jnp.zeros((64, 128), F32)
    wide = jnp.concatenate(
        [
            jnp.concatenate([jnp.where(low, left, zero), zero], 1),
            jnp.concatenate([jnp.where(low, zero, left), zero], 1),
            jnp.concatenate([zero, jnp.where(low, right, zero)], 1),
            jnp.concatenate([zero, jnp.where(low, zero, right)], 1),
        ],
        0,
    )
    return wide.astype(BF16), jnp.concatenate([over_left, over_right], 1)


def spatial_kernel(lat, mod, w_hbm, wo, out, xn, qkv, weights, ctx, w, wsems):
    copies = fetch(w_hbm, w, wsems)
    shift, scale, gate = mod[0:1, :], mod[1:2, :], mod[2:3, :]

    def norm_rows(i, carry):
        rows = pl.ds(pl.multiple_of(i * 64, 64), 64)
        xn[rows, :] = norm_mod(lat[rows, :].astype(F32), shift, scale)
        return carry

    lax.fori_loop(0, T // 64, norm_rows, 0, unroll=4)
    project_qkv(xn, w, copies, qkv)

    def attend(g, rows):
        for head in range(H):
            at = window(head)
            query = qkv[rows, at : at + WIN] * lane_mask(head, at, WIN)
            weights[head] = softmax_rows(mm_nt(query, qkv[rows, D + at : D + at + WIN]))
        for at, size in column_chunks(D, WIN):
            values = qkv[rows, 2 * D + at : 2 * D + at + size]
            mixed = 0
            for head in heads_of(at, size):
                mixed = mixed + mm(weights[head], values * lane_mask(head, at, size))
            ctx[rows, at : at + size] = mixed.astype(BF16)

    halves(attend)
    for at, size in column_chunks(D, WIN):
        cols = slice(at, at + size)
        parts = []
        for rows in (slice(0, S), slice(S, T)):
            value = lat[rows, cols].astype(F32) + gate[:, cols] * mm(ctx[rows, :], wo[:, cols])
            parts.append(value.reshape(32, 8, size))
        out[:, :, cols] = jnp.concatenate(parts, axis=1).astype(BF16)


def temporal_kernel(
    group, x, mod, w_hbm, wo_hbm, out, xn, qkv, weights, rest, over, v_t, ctx_t, wide, w, wo, wsems, sem
):
    copies = fetch(w_hbm, w, wsems)
    last = pltpu.make_async_copy(wo_hbm, wo, sem)
    last.start()
    shift, scale, gate = mod[3:4, :], mod[4:5, :], mod[5:6, :]

    def widen(i, carry):
        value = x[i].astype(F32)
        for j in range(LANES):
            wide[j, pl.ds(pl.multiple_of(i * 16, 16), 16), :] = value[:, j * 128 : j * 128 + 128]
        return carry

    lax.fori_loop(0, 32, widen, 0, unroll=4)
    for p in range(4):
        picked = pl.ds(4 * group + p, 64, stride=8)
        values = jnp.concatenate([wide[j, picked, :] for j in range(LANES)], axis=1)
        rows = slice(p * 64, p * 64 + 64)
        rest[rows, :] = values.astype(BF16)
        xn[rows, :] = norm_mod(values, shift, scale)
    project_qkv(xn, w, copies, qkv)
    eye = identity(WIN)
    for at, size in column_chunks(D, WIN):
        v_t[at : at + size, :] = mm_nt(eye[:size, :size], qkv[:, 2 * D + at : 2 * D + at + size])
    for head in range(H):
        at = window(head)
        query = qkv[:, at : at + WIN] * lane_mask(head, at, WIN)
        weights[head], over[head] = softmax_blocks(mm_nt(qkv[:, D + at : D + at + WIN], query))
    for head in range(H):
        mine = slice(head * HEAD, head * HEAD + HEAD)
        ctx_t[mine, :] = mm(v_t[mine, :].astype(BF16), weights[head]) * over[head]
    ctx = mm_nt(eye, ctx_t[...].astype(BF16)).astype(BF16)
    last.wait()
    for at, size in column_chunks(D, WIN):
        cols = slice(at, at + size)
        value = rest[:, cols].astype(F32) + gate[:, cols] * mm(ctx, wo[:, cols])
        for p in range(4):
            for j in range(size // 128):
                piece = value[p * 64 : p * 64 + 64, j * 128 : j * 128 + 128]
                wide[at // 128 + j, pl.ds(p, 64, stride=4), :] = piece

    def narrow(i, carry):
        rows = pl.ds(pl.multiple_of(i * 16, 16), 16)
        out[rows, :] = jnp.concatenate([wide[j, rows, :] for j in range(LANES)], axis=1).astype(BF16)
        return carry

    lax.fori_loop(0, 16, narrow, 0, unroll=4)


def assemble_kernel(place, *refs):
    pieces, (out, sem) = refs[:6], refs[6:]
    core, x_lo = place[1], place[2]

    def put(which, src, z, x):
        row = pl.multiple_of(z * (D // 2) + x * BLOCK, 16)
        pltpu.make_async_copy(src, out.at[which, pl.ds(row, BLOCK), :], sem).start()

    for own in range(2):
        which = core if own == 0 else 1 - core
        same, other_first, other_last = pieces[3 * own : 3 * own + 3]
        for z in range(2):
            put(which, same.at[0, z], z, x_lo)
            put(which, same.at[1, z], z, 2 + x_lo)
            put(which, other_first.at[z], z, 1 - x_lo)
            put(which, other_last.at[z], z, 3 - x_lo)
    pltpu.make_async_copy(out, out, sem).wait()


def cross_kernel(group, place, *refs):
    if group == 0:
        first, (x, keys, values, w, out, query, weights, over, v_t, ctx_t) = None, refs
    else:
        first, x, keys, values, w, out, query, weights, over, v_t, ctx_t = refs
    length = place[0]
    eye = identity(WIN)
    for at, size in column_chunks(D, WIN):
        v_t[at : at + size, :] = mm_nt(eye[:size, :size], values[:, at : at + size])
    for at, size in column_chunks(D, CHUNK):
        query[:, at : at + size] = mm(x[...], w[0, :, at : at + size]).astype(BF16)
    valid = lax.broadcasted_iota(jnp.int32, (SLOTS, S), 0) < length
    for head in range(H):
        at = window(head)
        masked = keys[:, at : at + WIN] * lane_mask(head, at, WIN)
        scores = mm_nt(masked, query[:, at : at + WIN])
        expo, over[head] = softmax_cols(jnp.where(valid, scores, -1e30))
        weights[head] = expo.astype(BF16)
    for head in range(H):
        mine = slice(head * HEAD, head * HEAD + HEAD)
        ctx_t[mine, :] = mm(v_t[mine, :].astype(BF16), weights[head]) * over[head]
    ctx = mm_nt(eye, ctx_t[...].astype(BF16)).astype(BF16)
    for at, size in column_chunks(D, WIN):
        cols = slice(at, at + size)
        value = x[:, cols].astype(F32) + mm(ctx, w[1, :, cols])
        if group == 0:
            out[:, cols] = value.astype(BF16)
            continue
        mine = value.reshape(32, 8, size)
        before = first[:, cols].astype(F32).reshape(32, 8, size)
        low = lax.broadcasted_iota(jnp.int32, (32, 8, size), 1) < 4
        frames = [
            jnp.where(low, before, pltpu.roll(mine, 4, 1)),
            jnp.where(low, pltpu.roll(before, 4, 1), mine),
        ]
        for f in range(2):
            out[f, :, cols] = frames[f].reshape(S, size).astype(BF16)


def vmem(*shape):
    return pltpu.VMEM(shape, BF16)


def call(kernel, name, shape, scratch, flops, transcendentals, spaces, *args):
    args = [
        pltpu.with_memory_space_constraint(arg, space) if space == pltpu.HBM else arg
        for arg, space in zip(args, spaces)
    ]
    return pl.pallas_call(
        kernel,
        out_shape=jax.ShapeDtypeStruct(shape, BF16),
        in_specs=[pl.BlockSpec(memory_space=pl.ANY if space == pltpu.HBM else space) for space in spaces],
        out_specs=pl.BlockSpec(memory_space=pltpu.VMEM),
        scratch_shapes=scratch,
        compiler_params=pltpu.CompilerParams(vmem_limit_bytes=32 * 1024 * 1024),
        cost_estimate=pl.CostEstimate(
            flops=flops, bytes_accessed=13_000_000, transcendentals=transcendentals
        ),
        name=name,
    )(*args)


def chunk_semaphores():
    return pltpu.SemaphoreType.DMA((len(column_chunks(3 * D, CHUNK)),))


def spatial(*args):
    scratch = [vmem(T, D), vmem(T, 3 * D), vmem(H, S, S), vmem(T, D), vmem(D, 3 * D), chunk_semaphores()]
    spaces = [pltpu.VMEM, pltpu.VMEM, pltpu.HBM, pltpu.VMEM]
    return call(spatial_kernel, "spatial", (32, 16, D), scratch, 8_000_000_000, 2_100_000, spaces, *args)


def temporal(group, *args):
    scratch = [
        vmem(S, D),
        vmem(S, 3 * D),
        vmem(H, S, S),
        vmem(S, D),
        pltpu.VMEM((H, 1, S), F32),
        pltpu.VMEM((D, S), F32),
        pltpu.VMEM((D, S), F32),
        pltpu.VMEM((LANES, T, 128), F32),
        vmem(D, 3 * D),
        vmem(D, D),
        chunk_semaphores(),
        pltpu.SemaphoreType.DMA,
    ]
    spaces = [pltpu.VMEM, pltpu.VMEM, pltpu.HBM, pltpu.HBM]
    kernel = functools.partial(temporal_kernel, group)
    name = f"temporal_{group}"
    return call(kernel, name, (S, D), scratch, 4_000_000_000, 300_000, spaces, *args)


def assemble(place, pieces):
    spaces = [pltpu.SMEM] + [pl.ANY] * len(pieces)
    scratch = [pltpu.SemaphoreType.DMA]
    return call(assemble_kernel, "assemble", (2, D, D), scratch, 0, 0, spaces, place, *pieces)


def cross(group, place, first, x, keys, values, w):
    scratch = [
        vmem(S, D),
        vmem(H, SLOTS, S),
        pltpu.VMEM((H, 1, S), F32),
        pltpu.VMEM((D, SLOTS), F32),
        pltpu.VMEM((D, S), F32),
    ]
    lead = [] if group == 0 else [first]
    args = [place, *lead, x, keys, values, w]
    spaces = [pltpu.SMEM] + [pltpu.VMEM] * (len(args) - 1)
    shape = (S, D) if group == 0 else (2, S, D)
    kernel = functools.partial(cross_kernel, group)
    name = f"cross_{group}"
    return call(kernel, name, shape, scratch, 2_000_000_000, 500_000, spaces, *args)


def shift(array, axes, by, size):
    return lax.ppermute(array, axes, [(i, (i + by) % size) for i in range(size)])


def over_seq(blocks):
    return lax.all_to_all(blocks, SEQ, split_axis=0, concat_axis=0, tiled=True)


def gather_even(rows):
    copies = jnp.broadcast_to(rows[None], (16,) + rows.shape)
    axes = ("x_hi", "z_lo", "y")
    found = lax.all_to_all(copies, axes, split_axis=0, concat_axis=0, tiled=True)
    return found


def body(
    latent,
    modulation,
    w_spatial_qkv,
    w_spatial_out,
    w_temporal_qkv,
    w_temporal_out,
    cross_query,
    cross_out,
    text_keys,
    text_values,
    text_len,
):
    mine = jnp.where(lax.axis_index("core") == 0, cross_query, cross_out)
    found = gather_even(mine)
    after_spatial = spatial(latent.reshape(T, D), modulation, w_spatial_qkv, w_spatial_out)
    found, after_spatial = lax.optimization_barrier((found, after_spatial))
    placed = over_seq(after_spatial)
    same = found.reshape(2, 2, BLOCK, D)
    same, placed = lax.optimization_barrier((same, placed))
    other_first = shift(same[0], ("x_hi", "x_lo"), 1, 4)
    other_last = shift(same[1], ("x_hi", "x_lo"), -1, 4)
    halves = [temporal(0, placed, modulation, w_temporal_qkv, w_temporal_out)]
    returned = [over_seq(halves[0].reshape(32, 8, D)).reshape(S, D)]
    placed, halves[0] = lax.optimization_barrier((placed, halves[0]))
    halves.append(temporal(1, placed, modulation, w_temporal_qkv, w_temporal_out))
    pieces = [same, other_first, other_last]
    pieces, halves[1] = lax.optimization_barrier((pieces, halves[1]))
    returned.append(over_seq(halves[1].reshape(32, 8, D)).reshape(S, D))
    pieces = pieces + [shift(piece, "core", 1, 2) for piece in pieces]
    place = jnp.stack([text_len[0], lax.axis_index("core"), lax.axis_index("x_lo")]).astype(jnp.int32)
    fill = ((0, SLOTS - text_keys.shape[0]), (0, 0))
    keys, values = jnp.pad(text_keys, fill), jnp.pad(text_values, fill)
    whole = assemble(place, pieces)
    first = cross(0, place, None, returned[0], keys, values, whole)
    return cross(1, place, first, returned[1], keys, values, whole)


def solution(mesh):
    fine = Mesh(mesh.devices.reshape(2, 2, 2, 4, 2, 2), SEQ + ("z_hi", "core"))
    part = ("z_hi", "core")
    placed = (
        P(ALL, None, None),
        P(part, None),
        P(),
        P(),
        P(),
        P(),
        P(SEQ, None),
        P(SEQ, None),
        P(part, None),
        P(part, None),
        P(part),
    )
    return jax.shard_map(
        body, mesh=fine, in_specs=placed, out_specs=P(ALL, None, None), check_vma=False
    )
```

```python
import jax
import jax.numpy as jnp
import numpy as np
from jax import lax
from jax.experimental import pallas as pl
from jax.experimental.pallas import tpu as pltpu
from jax.sharding import Mesh, PartitionSpec as P

H = 16
HEAD = 72
LANES = 9
D = 1152
S = 256
T = 512
WIN = 256
SLOTS = 128
BLOCK = 144
CHUNK = 512
EXP_SCALE = float(np.log2(np.e) / np.sqrt(72.0))
F32 = jnp.float32
BF16 = jnp.bfloat16
NT = (((1,), (1,)), ((), ()))
SEQ = ("z_lo", "x_hi", "x_lo", "y")
ALL = ("z_hi", "core") + SEQ


def mm(a, b):
    return jnp.dot(a, b, preferred_element_type=F32)


def mm_nt(a, b):
    return lax.dot_general(a, b, NT, preferred_element_type=F32)


def window(head):
    return min(HEAD * head // 128 * 128, D - WIN)


def lane_mask(head, at, size):
    lane = lax.broadcasted_iota(jnp.int32, (1, size), 1) + at
    inside = (lane >= HEAD * head) & (lane < HEAD * head + HEAD)
    return jnp.where(inside, 1.0, 0.0).astype(BF16)


def heads_of(at, size):
    return [h for h in range(H) if h * HEAD < at + size and h * HEAD + HEAD > at]


def identity(n):
    rows = lax.broadcasted_iota(jnp.int32, (n, n), 0)
    cols = lax.broadcasted_iota(jnp.int32, (n, n), 1)
    return jnp.where(rows == cols, 1.0, 0.0).astype(BF16)


def norm_mod(values, shift, scale):
    mean = jnp.mean(values, axis=-1, keepdims=True)
    centered = values - mean
    var = jnp.mean(centered * centered, axis=-1, keepdims=True)
    return (centered * lax.rsqrt(var + 1e-06) * (1.0 + scale) + shift).astype(BF16)


def column_chunks(width, chunk):
    return [(at, min(chunk, width - at)) for at in range(0, width, chunk)]


def halves(body):
    def step(g, carry):
        body(g, pl.ds(pl.multiple_of(g * S, S), S))
        return carry

    lax.fori_loop(0, 2, step, 0)


def fetch(src, dst, sems):
    copies = []
    for n, (at, size) in enumerate(column_chunks(src.shape[1], CHUNK)):
        cols = pl.ds(at, size)
        copies.append(pltpu.make_async_copy(src.at[:, cols], dst.at[:, cols], sems.at[n]))
        copies[-1].start()
    return copies


def project_qkv(xn, w, copies, qkv):
    for copy, (at, size) in zip(copies, column_chunks(3 * D, CHUNK)):
        copy.wait()
        for rows in (slice(0, S), slice(S, T)):
            qkv[rows, at : at + size] = mm(xn[rows, :], w[:, at : at + size]).astype(BF16)


def softmax_rows(scores):
    top = jnp.max(scores, axis=1, keepdims=True)
    expo = jnp.exp2(scores * EXP_SCALE - top * EXP_SCALE)
    return (expo * (1.0 / jnp.sum(expo, axis=1, keepdims=True))).astype(BF16)


def softmax_cols(scores):
    top = jnp.max(scores, axis=0, keepdims=True)
    expo = jnp.exp2(scores * EXP_SCALE - top * EXP_SCALE)
    return expo, 1.0 / jnp.sum(expo, axis=0, keepdims=True)


def softmax_blocks(scores):
    low = lax.broadcasted_iota(jnp.int32, (64, 128), 1) < 64
    left, over_left = softmax_cols(jnp.where(low, scores[0:64, :128], scores[64:128, :128]))
    right, over_right = softmax_cols(jnp.where(low, scores[128:192, 128:], scores[192:256, 128:]))
    zero = jnp.zeros((64, 128), F32)
    wide = jnp.concatenate(
        [
            jnp.concatenate([jnp.where(low, left, zero), zero], 1),
            jnp.concatenate([jnp.where(low, zero, left), zero], 1),
            jnp.concatenate([zero, jnp.where(low, right, zero)], 1),
            jnp.concatenate([zero, jnp.where(low, zero, right)], 1),
        ],
        0,
    )
    return wide.astype(BF16), jnp.concatenate([over_left, over_right], 1)


def spatial_kernel(lat, mod, w_hbm, wo_hbm, out, xn, qkv, weights, ctx, w, wo, sem, wsems):
    copies = fetch(w_hbm, w, wsems)
    last = pltpu.make_async_copy(wo_hbm, wo, sem)
    last.start()
    shift, scale, gate = mod[0:1, :], mod[1:2, :], mod[2:3, :]

    def norm_rows(i, carry):
        rows = pl.ds(pl.multiple_of(i * 64, 64), 64)
        xn[rows, :] = norm_mod(lat[rows, :].astype(F32), shift, scale)
        return carry

    lax.fori_loop(0, T // 64, norm_rows, 0, unroll=4)
    project_qkv(xn, w, copies, qkv)

    def attend(g, rows):
        for head in range(H):
            at = window(head)
            query = qkv[rows, at : at + WIN] * lane_mask(head, at, WIN)
            weights[head] = softmax_rows(mm_nt(query, qkv[rows, D + at : D + at + WIN]))
        for at, size in column_chunks(D, WIN):
            values = qkv[rows, 2 * D + at : 2 * D + at + size]
            mixed = 0
            for head in heads_of(at, size):
                mixed = mixed + mm(weights[head], values * lane_mask(head, at, size))
            ctx[rows, at : at + size] = mixed.astype(BF16)

    halves(attend)
    last.wait()
    for at, size in column_chunks(D, WIN):
        cols = slice(at, at + size)
        parts = []
        for rows in (slice(0, S), slice(S, T)):
            value = lat[rows, cols].astype(F32) + gate[:, cols] * mm(ctx[rows, :], wo[:, cols])
            parts.append(value.reshape(32, 8, size))
        out[:, :, cols] = jnp.concatenate(parts, axis=1).astype(BF16)


def temporal_kernel(
    x, mod, w_hbm, wo_hbm, out, xn, qkv, weights, ctx, rest, over, v_t, ctx_t, wide, w, wo, sem, wsems
):
    copies = fetch(w_hbm, w, wsems)
    last = pltpu.make_async_copy(wo_hbm, wo, sem)
    last.start()
    shift, scale, gate = mod[3:4, :], mod[4:5, :], mod[5:6, :]

    def widen(i, carry):
        value = x[i].astype(F32)
        for j in range(LANES):
            wide[j, pl.ds(pl.multiple_of(i * 16, 16), 16), :] = value[:, j * 128 : j * 128 + 128]
        return carry

    lax.fori_loop(0, 32, widen, 0, unroll=4)

    def norm_rows(p, carry):
        picked = pl.ds(p, 64, stride=8)
        values = jnp.concatenate([wide[j, picked, :] for j in range(LANES)], axis=1)
        rows = pl.ds(pl.multiple_of(p * 64, 64), 64)
        rest[rows, :] = values.astype(BF16)
        xn[rows, :] = norm_mod(values, shift, scale)
        return carry

    lax.fori_loop(0, 8, norm_rows, 0, unroll=4)
    project_qkv(xn, w, copies, qkv)
    eye = identity(WIN)

    def attend(g, rows):
        for at, size in column_chunks(D, WIN):
            v_t[at : at + size, :] = mm_nt(eye[:size, :size], qkv[rows, 2 * D + at : 2 * D + at + size])
        for head in range(H):
            at = window(head)
            query = qkv[rows, at : at + WIN] * lane_mask(head, at, WIN)
            weights[head], over[head] = softmax_blocks(mm_nt(qkv[rows, D + at : D + at + WIN], query))
        for head in range(H):
            mine = slice(head * HEAD, head * HEAD + HEAD)
            ctx_t[mine, :] = mm(v_t[mine, :].astype(BF16), weights[head]) * over[head]
        ctx[rows, :] = mm_nt(eye, ctx_t[...].astype(BF16)).astype(BF16)

    halves(attend)
    last.wait()
    for at, size in column_chunks(D, WIN):
        cols = slice(at, at + size)
        for g in range(2):
            rows = slice(g * S, g * S + S)
            value = rest[rows, cols].astype(F32) + gate[:, cols] * mm(ctx[rows, :], wo[:, cols])
            for p in range(4):
                for j in range(size // 128):
                    piece = value[p * 64 : p * 64 + 64, j * 128 : j * 128 + 128]
                    wide[at // 128 + j, pl.ds(g * 4 + p, 64, stride=8), :] = piece

    def narrow(i, carry):
        rows = pl.ds(pl.multiple_of(i * 16, 16), 16)
        out[i] = jnp.concatenate([wide[j, rows, :] for j in range(LANES)], axis=1).astype(BF16)
        return carry

    lax.fori_loop(0, 32, narrow, 0, unroll=4)


def cross_kernel(place, x, keys, values, *refs):
    pieces, (out, w, query, weights, over, v_t, ctx_t, ctx, sems) = refs[:16], refs[16:]
    length, core, z_lo, x_lo = place[0], place[1], place[2], place[3]

    def put_whole(which, source):
        for n, src in enumerate(pieces[8 * source : 8 * source + 8]):
            x_hi, side, z = n % 2, n // 4, n // 2 % 2
            x = 2 * x_hi + (x_lo if side == 0 else 1 - x_lo)
            row = (z_lo if z == 0 else 1 - z_lo) * (D // 2) + x * BLOCK
            rows = pl.ds(pl.multiple_of(row, 16), BLOCK)
            pltpu.make_async_copy(src, w.at[which, rows, :], sems.at[which]).start()

    for one in range(2):

        @pl.when(core == one)
        def _():
            put_whole(0, one)
            put_whole(1, 1 - one)

    def whole(which):
        pltpu.make_async_copy(w.at[which], w.at[which], sems.at[which]).wait()

    eye = identity(WIN)
    for at, size in column_chunks(D, WIN):
        v_t[at : at + size, :] = mm_nt(eye[:size, :size], values[:, at : at + size])
    whole(0)
    for at, size in column_chunks(D, CHUNK):
        for g in range(2):
            rows = x[g * 16 : g * 16 + 16].reshape(S, D)
            query[g * S : g * S + S, at : at + size] = mm(rows, w[0, :, at : at + size]).astype(BF16)
    valid = lax.broadcasted_iota(jnp.int32, (SLOTS, T), 0) < length
    for head in range(H):
        at = window(head)
        masked = keys[:, at : at + WIN] * lane_mask(head, at, WIN)
        scores = mm_nt(masked, query[:, at : at + WIN])
        expo, over[head] = softmax_cols(jnp.where(valid, scores, -1e30))
        weights[head] = expo.astype(BF16)
    for head in range(H):
        mine = slice(head * HEAD, head * HEAD + HEAD)
        ctx_t[mine, :] = mm(v_t[mine, :].astype(BF16), weights[head]) * over[head]
    for g in range(2):
        rows = slice(g * S, g * S + S)
        ctx[rows, :] = mm_nt(eye, ctx_t[:, rows].astype(BF16)).astype(BF16)
    whole(1)
    for at, size in column_chunks(D, WIN):
        cols = slice(at, at + size)
        for g in range(2):
            value = x[g * 16 : g * 16 + 16, :, cols].astype(F32).reshape(S, size)
            value = value + mm(ctx[g * S : g * S + S, :], w[1, :, cols])
            value = value.reshape(16, 2, 8, size)
            for f in range(2):
                out[f, g * 128 : g * 128 + 128, cols] = value[:, f].reshape(128, size).astype(BF16)


def vmem(*shape):
    return pltpu.VMEM(shape, BF16)


def weight_scratch():
    n = len(column_chunks(3 * D, CHUNK))
    return [
        vmem(D, 3 * D),
        vmem(D, D),
        pltpu.SemaphoreType.DMA,
        pltpu.SemaphoreType.DMA((n,)),
    ]


def call(kernel, name, shape, scratch, flops, transcendentals, spaces, *args):
    args = [
        pltpu.with_memory_space_constraint(arg, space) if space == pltpu.HBM else arg
        for arg, space in zip(args, spaces)
    ]
    return pl.pallas_call(
        kernel,
        out_shape=jax.ShapeDtypeStruct(shape, BF16),
        in_specs=[pl.BlockSpec(memory_space=pl.ANY if space == pltpu.HBM else space) for space in spaces],
        out_specs=pl.BlockSpec(memory_space=pltpu.VMEM),
        scratch_shapes=scratch,
        compiler_params=pltpu.CompilerParams(vmem_limit_bytes=34 * 1024 * 1024),
        cost_estimate=pl.CostEstimate(
            flops=flops, bytes_accessed=13_000_000, transcendentals=transcendentals
        ),
        name=name,
    )(*args)


def spatial(*args):
    scratch = [vmem(T, D), vmem(T, 3 * D), vmem(H, S, S), vmem(T, D)]
    scratch = scratch + weight_scratch()
    spaces = [pltpu.VMEM, pltpu.VMEM, pltpu.HBM, pltpu.HBM]
    return call(spatial_kernel, "spatial", (32, 16, D), scratch, 8_000_000_000, 2_100_000, spaces, *args)


def temporal(*args):
    scratch = [
        vmem(T, D),
        vmem(T, 3 * D),
        vmem(H, S, S),
        vmem(T, D),
        vmem(T, D),
        pltpu.VMEM((H, 1, S), F32),
        pltpu.VMEM((D, S), F32),
        pltpu.VMEM((D, S), F32),
        pltpu.VMEM((LANES, T, 128), F32),
    ]
    scratch = scratch + weight_scratch()
    spaces = [pltpu.VMEM, pltpu.VMEM, pltpu.HBM, pltpu.HBM]
    return call(temporal_kernel, "temporal", (32, 16, D), scratch, 8_000_000_000, 600_000, spaces, *args)


def cross(place, x, keys, values, pieces):
    scratch = [
        vmem(2, D, D),
        vmem(T, D),
        vmem(H, SLOTS, T),
        pltpu.VMEM((H, 1, T), F32),
        pltpu.VMEM((D, SLOTS), F32),
        pltpu.VMEM((D, T), F32),
        vmem(T, D),
        pltpu.SemaphoreType.DMA((2,)),
    ]
    args = (place, x, keys, values, *pieces)
    spaces = [pltpu.SMEM] + [pltpu.VMEM] * 3 + [pltpu.HBM] * len(pieces)
    return call(cross_kernel, "cross", (2, S, D), scratch, 4_000_000_000, 1_000_000, spaces, *args)


def shift(array, axes, by, size):
    return lax.ppermute(array, axes, [(i, (i + by) % size) for i in range(size)])


def gather_even(first, last):
    shape = (8,) + first.shape
    copies = jnp.where(
        lax.axis_index("core") == 0,
        jnp.broadcast_to(first[None], shape),
        jnp.broadcast_to(last[None], shape),
    )
    return lax.all_to_all(copies, ("x_hi", "y"), split_axis=0, concat_axis=0, tiled=True)


def over_z(block):
    return lax.ppermute(block, ("z_lo", "z_hi"), [(i, 3 - i) for i in range(4)])


def body(
    latent,
    modulation,
    w_spatial_qkv,
    w_spatial_out,
    w_temporal_qkv,
    w_temporal_out,
    cross_query,
    cross_out,
    text_keys,
    text_values,
    text_len,
):
    found = gather_even(cross_query, cross_out)
    after_spatial = spatial(latent.reshape(T, D), modulation, w_spatial_qkv, w_spatial_out)
    found, after_spatial = lax.optimization_barrier((found, after_spatial))
    placed = lax.all_to_all(after_spatial, SEQ, split_axis=0, concat_axis=0, tiled=True)
    own = [found[:4].reshape(BLOCK, D), found[4:].reshape(BLOCK, D)]
    others = [over_z(block) for block in own]
    own, others, placed = lax.optimization_barrier((own, others, placed))
    sides = [shift(own[n], ("x_hi", "x_lo"), (1, -1)[n], 4) for n in range(2)]
    far_side = shift(others[0], ("x_hi", "x_lo"), 1, 4)
    after_temporal = temporal(placed, modulation, w_temporal_qkv, w_temporal_out)
    sides, far_side, after_temporal = lax.optimization_barrier((sides, far_side, after_temporal))
    returned = lax.all_to_all(after_temporal, SEQ, split_axis=0, concat_axis=0, tiled=True)
    pieces = own + others + sides + [far_side, over_z(sides[1])]
    pieces = pieces + [shift(piece, "core", 1, 2) for piece in pieces]
    place = jnp.stack(
        [text_len[0], lax.axis_index("core"), lax.axis_index("z_lo"), lax.axis_index("x_lo")]
    ).astype(jnp.int32)
    fill = ((0, SLOTS - text_keys.shape[0]), (0, 0))
    keys, values = jnp.pad(text_keys, fill), jnp.pad(text_values, fill)
    return cross(place, returned, keys, values, pieces)


def solution(mesh):
    fine = Mesh(mesh.devices.reshape(2, 2, 2, 4, 2, 2), SEQ + ("z_hi", "core"))
    part = ("z_hi", "core")
    placed = (
        P(ALL, None, None),
        P(part, None),
        P(),
        P(),
        P(),
        P(),
        P(SEQ, None),
        P(SEQ, None),
        P(part, None),
        P(part, None),
        P(part),
    )
    return jax.shard_map(
        body, mesh=fine, in_specs=placed, out_specs=P(ALL, None, None), check_vma=False
    )
```

```python
import jax
import jax.numpy as jnp
import numpy as np
from jax import lax
from jax.experimental import pallas as pl
from jax.experimental.pallas import tpu as pltpu
from jax.sharding import Mesh, PartitionSpec as P

H = 16
HEAD = 72
LANES = 9
D = 1152
S = 256
T = 512
WIN = 256
SLOTS = 128
BLOCK = 144
CHUNK = 512
EXP_SCALE = float(np.log2(np.e) / np.sqrt(72.0))
F32 = jnp.float32
BF16 = jnp.bfloat16
NT = (((1,), (1,)), ((), ()))
SEQ = ("z_lo", "x_hi", "x_lo", "y")
ALL = ("z_hi", "core") + SEQ


def mm(a, b):
    return jnp.dot(a, b, preferred_element_type=F32)


def mm_nt(a, b):
    return lax.dot_general(a, b, NT, preferred_element_type=F32)


def window(head):
    return min(HEAD * head // 128 * 128, D - WIN)


def lane_mask(head, at, size):
    lane = lax.broadcasted_iota(jnp.int32, (1, size), 1) + at
    inside = (lane >= HEAD * head) & (lane < HEAD * head + HEAD)
    return jnp.where(inside, 1.0, 0.0).astype(BF16)


def heads_of(at, size):
    return [h for h in range(H) if h * HEAD < at + size and h * HEAD + HEAD > at]


def identity(n):
    rows = lax.broadcasted_iota(jnp.int32, (n, n), 0)
    cols = lax.broadcasted_iota(jnp.int32, (n, n), 1)
    return jnp.where(rows == cols, 1.0, 0.0).astype(BF16)


def norm_mod(values, shift, scale):
    mean = jnp.mean(values, axis=-1, keepdims=True)
    centered = values - mean
    var = jnp.mean(centered * centered, axis=-1, keepdims=True)
    return (centered * lax.rsqrt(var + 1e-06) * (1.0 + scale) + shift).astype(BF16)


def column_chunks(width, chunk):
    return [(at, min(chunk, width - at)) for at in range(0, width, chunk)]


def halves(body):
    for rows in (slice(0, S), slice(S, T)):
        body(rows)


def fetch(src, dst, sems):
    copies = []
    for n, (at, size) in enumerate(column_chunks(src.shape[1], CHUNK)):
        cols = pl.ds(at, size)
        copies.append(pltpu.make_async_copy(src.at[:, cols], dst.at[:, cols], sems.at[n]))
        copies[-1].start()
    return copies


def project_qkv(xn, w, copies, qkv):
    for copy, (at, size) in zip(copies, column_chunks(3 * D, CHUNK)):
        copy.wait()
        for rows in (slice(0, S), slice(S, T)):
            qkv[rows, at : at + size] = mm(xn[rows, :], w[:, at : at + size]).astype(BF16)


def softmax_rows(scores):
    top = jnp.max(scores, axis=1, keepdims=True)
    expo = jnp.exp2(scores * EXP_SCALE - top * EXP_SCALE)
    return (expo * (1.0 / jnp.sum(expo, axis=1, keepdims=True))).astype(BF16)


def softmax_cols(scores):
    top = jnp.max(scores, axis=0, keepdims=True)
    expo = jnp.exp2(scores * EXP_SCALE - top * EXP_SCALE)
    return expo, 1.0 / jnp.sum(expo, axis=0, keepdims=True)


def softmax_blocks(scores):
    low = lax.broadcasted_iota(jnp.int32, (64, 128), 1) < 64
    left, over_left = softmax_cols(jnp.where(low, scores[0:64, :128], scores[64:128, :128]))
    right, over_right = softmax_cols(jnp.where(low, scores[128:192, 128:], scores[192:256, 128:]))
    zero = jnp.zeros((64, 128), F32)
    wide = jnp.concatenate(
        [
            jnp.concatenate([jnp.where(low, left, zero), zero], 1),
            jnp.concatenate([jnp.where(low, zero, left), zero], 1),
            jnp.concatenate([zero, jnp.where(low, right, zero)], 1),
            jnp.concatenate([zero, jnp.where(low, zero, right)], 1),
        ],
        0,
    )
    return wide.astype(BF16), jnp.concatenate([over_left, over_right], 1)


def spatial_kernel(lat, mod, w_hbm, wo_hbm, out, xn, qkv, weights, ctx, w, wo, sem, wsems):
    copies = fetch(w_hbm, w, wsems)
    last = pltpu.make_async_copy(wo_hbm, wo, sem)
    last.start()
    shift, scale, gate = mod[0:1, :], mod[1:2, :], mod[2:3, :]

    def norm_rows(i, carry):
        rows = pl.ds(pl.multiple_of(i * 64, 64), 64)
        xn[rows, :] = norm_mod(lat[rows, :].astype(F32), shift, scale)
        return carry

    lax.fori_loop(0, T // 64, norm_rows, 0, unroll=4)
    project_qkv(xn, w, copies, qkv)

    def attend(rows):
        for head in range(H):
            at = window(head)
            query = qkv[rows, at : at + WIN] * lane_mask(head, at, WIN)
            weights[head] = softmax_rows(mm_nt(query, qkv[rows, D + at : D + at + WIN]))
        for at, size in column_chunks(D, WIN):
            values = qkv[rows, 2 * D + at : 2 * D + at + size]
            mixed = 0
            for head in heads_of(at, size):
                mixed = mixed + mm(weights[head], values * lane_mask(head, at, size))
            ctx[rows, at : at + size] = mixed.astype(BF16)

    halves(attend)
    last.wait()
    for at, size in column_chunks(D, WIN):
        cols = slice(at, at + size)
        parts = []
        for rows in (slice(0, S), slice(S, T)):
            value = lat[rows, cols].astype(F32) + gate[:, cols] * mm(ctx[rows, :], wo[:, cols])
            parts.append(value.reshape(32, 8, size))
        out[:, :, cols] = jnp.concatenate(parts, axis=1).astype(BF16)


def temporal_kernel(
    x, mod, w_hbm, wo_hbm, out, xn, qkv, weights, ctx, rest, over, v_t, ctx_t, wide, w, wo, sem, wsems
):
    copies = fetch(w_hbm, w, wsems)
    last = pltpu.make_async_copy(wo_hbm, wo, sem)
    last.start()
    shift, scale, gate = mod[3:4, :], mod[4:5, :], mod[5:6, :]

    def widen(i, carry):
        value = x[i].astype(F32)
        for j in range(LANES):
            wide[j, pl.ds(pl.multiple_of(i * 16, 16), 16), :] = value[:, j * 128 : j * 128 + 128]
        return carry

    lax.fori_loop(0, 32, widen, 0, unroll=4)

    def norm_rows(p, carry):
        picked = pl.ds(p, 64, stride=8)
        values = jnp.concatenate([wide[j, picked, :] for j in range(LANES)], axis=1)
        rows = pl.ds(pl.multiple_of(p * 64, 64), 64)
        rest[rows, :] = values.astype(BF16)
        xn[rows, :] = norm_mod(values, shift, scale)
        return carry

    lax.fori_loop(0, 8, norm_rows, 0, unroll=4)
    project_qkv(xn, w, copies, qkv)
    eye = identity(WIN)

    def attend(rows):
        for at, size in column_chunks(D, WIN):
            v_t[at : at + size, :] = mm_nt(eye[:size, :size], qkv[rows, 2 * D + at : 2 * D + at + size])
        for head in range(H):
            at = window(head)
            query = qkv[rows, at : at + WIN] * lane_mask(head, at, WIN)
            weights[head], over[head] = softmax_blocks(mm_nt(qkv[rows, D + at : D + at + WIN], query))
        for head in range(H):
            mine = slice(head * HEAD, head * HEAD + HEAD)
            ctx_t[mine, :] = mm(v_t[mine, :].astype(BF16), weights[head]) * over[head]
        ctx[rows, :] = mm_nt(eye, ctx_t[...].astype(BF16)).astype(BF16)

    halves(attend)
    last.wait()
    for at, size in column_chunks(D, WIN):
        cols = slice(at, at + size)
        for g in range(2):
            rows = slice(g * S, g * S + S)
            value = rest[rows, cols].astype(F32) + gate[:, cols] * mm(ctx[rows, :], wo[:, cols])
            for p in range(4):
                for j in range(size // 128):
                    piece = value[p * 64 : p * 64 + 64, j * 128 : j * 128 + 128]
                    wide[at // 128 + j, pl.ds(g * 4 + p, 64, stride=8), :] = piece

    def narrow(i, carry):
        rows = pl.ds(pl.multiple_of(i * 16, 16), 16)
        out[i] = jnp.concatenate([wide[j, rows, :] for j in range(LANES)], axis=1).astype(BF16)
        return carry

    lax.fori_loop(0, 32, narrow, 0, unroll=4)


def cross_kernel(place, x, keys, values, *refs):
    pieces, (out, w, query, weights, over, v_t, ctx_t, ctx, sems) = refs[:16], refs[16:]
    length, core, z_lo, x_lo = place[0], place[1], place[2], place[3]

    def put_whole(which, source):
        for n, src in enumerate(pieces[8 * source : 8 * source + 8]):
            x_hi, side, z = n % 2, n // 4, n // 2 % 2
            x = 2 * x_hi + (x_lo if side == 0 else 1 - x_lo)
            row = (z_lo if z == 0 else 1 - z_lo) * (D // 2) + x * BLOCK
            rows = pl.ds(pl.multiple_of(row, 16), BLOCK)
            pltpu.make_async_copy(src, w.at[which, rows, :], sems.at[which]).start()

    for one in range(2):

        @pl.when(core == one)
        def _():
            put_whole(0, one)
            put_whole(1, 1 - one)

    def whole(which):
        pltpu.make_async_copy(w.at[which], w.at[which], sems.at[which]).wait()

    eye = identity(WIN)
    for at, size in column_chunks(D, WIN):
        v_t[at : at + size, :] = mm_nt(eye[:size, :size], values[:, at : at + size])
    whole(0)
    for at, size in column_chunks(D, CHUNK):
        for g in range(2):
            rows = x[g * 16 : g * 16 + 16].reshape(S, D)
            query[g * S : g * S + S, at : at + size] = mm(rows, w[0, :, at : at + size]).astype(BF16)
    valid = lax.broadcasted_iota(jnp.int32, (SLOTS, T), 0) < length
    for head in range(H):
        at = window(head)
        masked = keys[:, at : at + WIN] * lane_mask(head, at, WIN)
        scores = mm_nt(masked, query[:, at : at + WIN])
        expo, over[head] = softmax_cols(jnp.where(valid, scores, -1e30))
        weights[head] = expo.astype(BF16)
    for head in range(H):
        mine = slice(head * HEAD, head * HEAD + HEAD)
        ctx_t[mine, :] = mm(v_t[mine, :].astype(BF16), weights[head]) * over[head]
    for g in range(2):
        rows = slice(g * S, g * S + S)
        ctx[rows, :] = mm_nt(eye, ctx_t[:, rows].astype(BF16)).astype(BF16)
    whole(1)
    for at, size in column_chunks(D, WIN):
        cols = slice(at, at + size)
        for g in range(2):
            value = x[g * 16 : g * 16 + 16, :, cols].astype(F32).reshape(S, size)
            value = value + mm(ctx[g * S : g * S + S, :], w[1, :, cols])
            value = value.reshape(16, 2, 8, size)
            for f in range(2):
                out[f, g * 128 : g * 128 + 128, cols] = value[:, f].reshape(128, size).astype(BF16)


def vmem(*shape):
    return pltpu.VMEM(shape, BF16)


def weight_scratch():
    n = len(column_chunks(3 * D, CHUNK))
    return [
        vmem(D, 3 * D),
        vmem(D, D),
        pltpu.SemaphoreType.DMA,
        pltpu.SemaphoreType.DMA((n,)),
    ]


def call(kernel, name, shape, scratch, mebibytes, flops, transcendentals, spaces, *args):
    args = [
        pltpu.with_memory_space_constraint(arg, space) if space == pltpu.HBM else arg
        for arg, space in zip(args, spaces)
    ]
    return pl.pallas_call(
        kernel,
        out_shape=jax.ShapeDtypeStruct(shape, BF16),
        in_specs=[pl.BlockSpec(memory_space=pl.ANY if space == pltpu.HBM else space) for space in spaces],
        out_specs=pl.BlockSpec(memory_space=pltpu.VMEM),
        scratch_shapes=scratch,
        compiler_params=pltpu.CompilerParams(vmem_limit_bytes=mebibytes * 1024 * 1024),
        cost_estimate=pl.CostEstimate(
            flops=flops, bytes_accessed=13_000_000, transcendentals=transcendentals
        ),
        name=name,
    )(*args)


def spatial(*args):
    scratch = [vmem(T, D), vmem(T, 3 * D), vmem(H, S, S), vmem(T, D)]
    scratch = scratch + weight_scratch()
    spaces = [pltpu.VMEM, pltpu.VMEM, pltpu.HBM, pltpu.HBM]
    return call(spatial_kernel, "spatial", (32, 16, D), scratch, 22, 8_000_000_000, 2_100_000, spaces, *args)


def temporal(*args):
    scratch = [
        vmem(T, D),
        vmem(T, 3 * D),
        vmem(H, S, S),
        vmem(T, D),
        vmem(T, D),
        pltpu.VMEM((H, 1, S), F32),
        pltpu.VMEM((D, S), F32),
        pltpu.VMEM((D, S), F32),
        pltpu.VMEM((LANES, T, 128), F32),
    ]
    scratch = scratch + weight_scratch()
    spaces = [pltpu.VMEM, pltpu.VMEM, pltpu.HBM, pltpu.HBM]
    return call(temporal_kernel, "temporal", (32, 16, D), scratch, 28, 8_000_000_000, 600_000, spaces, *args)


def cross(place, x, keys, values, pieces):
    scratch = [
        vmem(2, D, D),
        vmem(T, D),
        vmem(H, SLOTS, T),
        pltpu.VMEM((H, 1, T), F32),
        pltpu.VMEM((D, SLOTS), F32),
        pltpu.VMEM((D, T), F32),
        vmem(T, D),
        pltpu.SemaphoreType.DMA((2,)),
    ]
    args = (place, x, keys, values, *pieces)
    spaces = [pltpu.SMEM] + [pltpu.VMEM] * 3 + [pltpu.HBM] * len(pieces)
    return call(cross_kernel, "cross", (2, S, D), scratch, 16, 4_000_000_000, 1_000_000, spaces, *args)


def shift(array, axes, by, size):
    return lax.ppermute(array, axes, [(i, (i + by) % size) for i in range(size)])


def gather_even(first, last):
    shape = (8,) + first.shape
    copies = jnp.where(
        lax.axis_index("core") == 0,
        jnp.broadcast_to(first[None], shape),
        jnp.broadcast_to(last[None], shape),
    )
    return lax.all_to_all(copies, ("x_hi", "y"), split_axis=0, concat_axis=0, tiled=True)


def over_core(block):
    return shift(block, "core", 1, 2)


def over_z(block):
    return lax.ppermute(block, ("z_lo", "z_hi"), [(i, 3 - i) for i in range(4)])


def body(
    latent,
    modulation,
    w_spatial_qkv,
    w_spatial_out,
    w_temporal_qkv,
    w_temporal_out,
    cross_query,
    cross_out,
    text_keys,
    text_values,
    text_len,
):
    found = gather_even(cross_query, cross_out)
    after_spatial = spatial(latent.reshape(T, D), modulation, w_spatial_qkv, w_spatial_out)
    found, after_spatial = lax.optimization_barrier((found, after_spatial))
    placed = lax.all_to_all(after_spatial, SEQ, split_axis=0, concat_axis=0, tiled=True)
    own = [found[:4].reshape(BLOCK, D), found[4:].reshape(BLOCK, D)]
    others = [over_z(block) for block in own]
    own_swapped = [over_core(block) for block in own]
    own, own_swapped, others, placed = lax.optimization_barrier((own, own_swapped, others, placed))
    sides = [shift(own[n], ("x_hi", "x_lo"), (1, -1)[n], 4) for n in range(2)]
    far_side = shift(others[0], ("x_hi", "x_lo"), 1, 4)
    after_temporal = temporal(placed, modulation, w_temporal_qkv, w_temporal_out)
    sides, far_side, after_temporal = lax.optimization_barrier((sides, far_side, after_temporal))
    returned = lax.all_to_all(after_temporal, SEQ, split_axis=0, concat_axis=0, tiled=True)
    later = others + sides + [far_side, over_z(sides[1])]
    pieces = own + later + own_swapped + [over_core(block) for block in later]
    place = jnp.stack(
        [text_len[0], lax.axis_index("core"), lax.axis_index("z_lo"), lax.axis_index("x_lo")]
    ).astype(jnp.int32)
    fill = ((0, SLOTS - text_keys.shape[0]), (0, 0))
    keys, values = jnp.pad(text_keys, fill), jnp.pad(text_values, fill)
    return cross(place, returned, keys, values, pieces)


def solution(mesh):
    fine = Mesh(mesh.devices.reshape(2, 2, 2, 4, 2, 2), SEQ + ("z_hi", "core"))
    part = ("z_hi", "core")
    placed = (
        P(ALL, None, None),
        P(part, None),
        P(),
        P(),
        P(),
        P(),
        P(SEQ, None),
        P(SEQ, None),
        P(part, None),
        P(part, None),
        P(part),
    )
    return jax.shard_map(
        body, mesh=fine, in_specs=placed, out_specs=P(ALL, None, None), check_vma=False
    )
```

```python
import jax
import jax.numpy as jnp
import numpy as np
from jax import lax
from jax.experimental import pallas as pl
from jax.experimental.pallas import tpu as pltpu
from jax.sharding import Mesh, PartitionSpec as P

H = 16
HEAD = 72
LANES = 9
D = 1152
S = 256
T = 512
WIN = 256
SLOTS = 128
BLOCK = 144
CHUNK = 512
EXP_SCALE = float(np.log2(np.e) / np.sqrt(72.0))
F32 = jnp.float32
BF16 = jnp.bfloat16
NT = (((1,), (1,)), ((), ()))
SEQ = ("z_lo", "x_hi", "x_lo", "y")
ALL = ("z_hi", "core") + SEQ


def mm(a, b):
    return jnp.dot(a, b, preferred_element_type=F32)


def mm_nt(a, b):
    return lax.dot_general(a, b, NT, preferred_element_type=F32)


def window(head):
    return min(HEAD * head // 128 * 128, D - WIN)


def lane_mask(head, at, size):
    lane = lax.broadcasted_iota(jnp.int32, (1, size), 1) + at
    inside = (lane >= HEAD * head) & (lane < HEAD * head + HEAD)
    return jnp.where(inside, 1.0, 0.0).astype(BF16)


def heads_of(at, size):
    return [h for h in range(H) if h * HEAD < at + size and h * HEAD + HEAD > at]


def identity(n):
    rows = lax.broadcasted_iota(jnp.int32, (n, n), 0)
    cols = lax.broadcasted_iota(jnp.int32, (n, n), 1)
    return jnp.where(rows == cols, 1.0, 0.0).astype(BF16)


def norm_mod(values, shift, scale):
    mean = jnp.mean(values, axis=-1, keepdims=True)
    centered = values - mean
    var = jnp.mean(centered * centered, axis=-1, keepdims=True)
    return (centered * lax.rsqrt(var + 1e-06) * (1.0 + scale) + shift).astype(BF16)


def column_chunks(width, chunk):
    return [(at, min(chunk, width - at)) for at in range(0, width, chunk)]


def halves(body):
    for rows in (slice(0, S), slice(S, T)):
        body(rows)


def fetch(src, dst, sems):
    copies = []
    for n, (at, size) in enumerate(column_chunks(src.shape[1], CHUNK)):
        cols = pl.ds(at, size)
        copies.append(pltpu.make_async_copy(src.at[:, cols], dst.at[:, cols], sems.at[n]))
        copies[-1].start()
    return copies


def project_qkv(xn, w, copies, qkv):
    for copy, (at, size) in zip(copies, column_chunks(3 * D, CHUNK)):
        copy.wait()
        for rows in (slice(0, S), slice(S, T)):
            qkv[rows, at : at + size] = mm(xn[rows, :], w[:, at : at + size]).astype(BF16)


def softmax_rows(scores):
    top = jnp.max(scores, axis=1, keepdims=True)
    expo = jnp.exp2(scores * EXP_SCALE - top * EXP_SCALE)
    return (expo * (1.0 / jnp.sum(expo, axis=1, keepdims=True))).astype(BF16)


def softmax_cols(scores):
    top = jnp.max(scores, axis=0, keepdims=True)
    expo = jnp.exp2(scores * EXP_SCALE - top * EXP_SCALE)
    return expo, 1.0 / jnp.sum(expo, axis=0, keepdims=True)


def softmax_blocks(scores):
    low = lax.broadcasted_iota(jnp.int32, (64, 128), 1) < 64
    left, over_left = softmax_cols(jnp.where(low, scores[0:64, :128], scores[64:128, :128]))
    right, over_right = softmax_cols(jnp.where(low, scores[128:192, 128:], scores[192:256, 128:]))
    zero = jnp.zeros((64, 128), F32)
    wide = jnp.concatenate(
        [
            jnp.concatenate([jnp.where(low, left, zero), zero], 1),
            jnp.concatenate([jnp.where(low, zero, left), zero], 1),
            jnp.concatenate([zero, jnp.where(low, right, zero)], 1),
            jnp.concatenate([zero, jnp.where(low, zero, right)], 1),
        ],
        0,
    )
    return wide.astype(BF16), jnp.concatenate([over_left, over_right], 1)


def spatial_kernel(lat, mod, w_hbm, wo_hbm, out, xn, qkv, weights, ctx, w, wo, sem, wsems):
    copies = fetch(w_hbm, w, wsems)
    last = pltpu.make_async_copy(wo_hbm, wo, sem)
    last.start()
    shift, scale, gate = mod[0:1, :], mod[1:2, :], mod[2:3, :]

    def norm_rows(i, carry):
        rows = pl.ds(pl.multiple_of(i * 64, 64), 64)
        xn[rows, :] = norm_mod(lat[rows, :].astype(F32), shift, scale)
        return carry

    lax.fori_loop(0, T // 64, norm_rows, 0, unroll=4)
    project_qkv(xn, w, copies, qkv)

    def attend(rows):
        for head in range(H):
            at = window(head)
            query = qkv[rows, at : at + WIN] * lane_mask(head, at, WIN)
            weights[head] = softmax_rows(mm_nt(query, qkv[rows, D + at : D + at + WIN]))
        for at, size in column_chunks(D, WIN):
            values = qkv[rows, 2 * D + at : 2 * D + at + size]
            mixed = 0
            for head in heads_of(at, size):
                mixed = mixed + mm(weights[head], values * lane_mask(head, at, size))
            ctx[rows, at : at + size] = mixed.astype(BF16)

    halves(attend)
    last.wait()
    for at, size in column_chunks(D, WIN):
        cols = slice(at, at + size)
        parts = []
        for rows in (slice(0, S), slice(S, T)):
            value = lat[rows, cols].astype(F32) + gate[:, cols] * mm(ctx[rows, :], wo[:, cols])
            parts.append(value.reshape(32, 8, size))
        out[:, :, cols] = jnp.concatenate(parts, axis=1).astype(BF16)


def temporal_kernel(
    x, mod, w_hbm, wo_hbm, out, xn, qkv, weights, ctx, rest, over, v_t, ctx_t, wide, w, wo, sem, wsems
):
    copies = fetch(w_hbm, w, wsems)
    last = pltpu.make_async_copy(wo_hbm, wo, sem)
    last.start()
    shift, scale, gate = mod[3:4, :], mod[4:5, :], mod[5:6, :]

    def widen(i, carry):
        value = x[i].astype(F32)
        for j in range(LANES):
            wide[j, pl.ds(pl.multiple_of(i * 16, 16), 16), :] = value[:, j * 128 : j * 128 + 128]
        return carry

    lax.fori_loop(0, 32, widen, 0, unroll=4)

    def norm_rows(p, carry):
        picked = pl.ds(p, 64, stride=8)
        values = jnp.concatenate([wide[j, picked, :] for j in range(LANES)], axis=1)
        rows = pl.ds(pl.multiple_of(p * 64, 64), 64)
        rest[rows, :] = values.astype(BF16)
        xn[rows, :] = norm_mod(values, shift, scale)
        return carry

    lax.fori_loop(0, 8, norm_rows, 0, unroll=4)
    project_qkv(xn, w, copies, qkv)
    eye = identity(WIN)

    def attend(rows):
        for at, size in column_chunks(D, WIN):
            v_t[at : at + size, :] = mm_nt(eye[:size, :size], qkv[rows, 2 * D + at : 2 * D + at + size])
        for head in range(H):
            at = window(head)
            query = qkv[rows, at : at + WIN] * lane_mask(head, at, WIN)
            weights[head], over[head] = softmax_blocks(mm_nt(qkv[rows, D + at : D + at + WIN], query))
        for head in range(H):
            mine = slice(head * HEAD, head * HEAD + HEAD)
            ctx_t[mine, :] = mm(v_t[mine, :].astype(BF16), weights[head]) * over[head]
        ctx[rows, :] = mm_nt(eye, ctx_t[...].astype(BF16)).astype(BF16)

    halves(attend)
    last.wait()
    for at, size in column_chunks(D, WIN):
        cols = slice(at, at + size)
        for g in range(2):
            rows = slice(g * S, g * S + S)
            value = rest[rows, cols].astype(F32) + gate[:, cols] * mm(ctx[rows, :], wo[:, cols])
            for p in range(4):
                for j in range(size // 128):
                    piece = value[p * 64 : p * 64 + 64, j * 128 : j * 128 + 128]
                    wide[at // 128 + j, pl.ds(g * 4 + p, 64, stride=8), :] = piece

    def narrow(i, carry):
        rows = pl.ds(pl.multiple_of(i * 16, 16), 16)
        out[i] = jnp.concatenate([wide[j, rows, :] for j in range(LANES)], axis=1).astype(BF16)
        return carry

    lax.fori_loop(0, 32, narrow, 0, unroll=4)


def cross_kernel(place, x, keys, values, *refs):
    pieces, (out, w, query, weights, over, v_t, ctx_t, ctx, sems) = refs[:16], refs[16:]
    length, core, z_lo, x_lo = place[0], place[1], place[2], place[3]

    def put_whole(which, source):
        for n, src in enumerate(pieces[8 * source : 8 * source + 8]):
            x_hi, side, z = n % 2, n // 4, n // 2 % 2
            x = 2 * x_hi + (x_lo if side == 0 else 1 - x_lo)
            row = (z_lo if z == 0 else 1 - z_lo) * (D // 2) + x * BLOCK
            rows = pl.ds(pl.multiple_of(row, 16), BLOCK)
            pltpu.make_async_copy(src, w.at[which, rows, :], sems.at[which]).start()

    for one in range(2):

        @pl.when(core == one)
        def _():
            put_whole(0, one)
            put_whole(1, 1 - one)

    def whole(which):
        pltpu.make_async_copy(w.at[which], w.at[which], sems.at[which]).wait()

    eye = identity(WIN)
    for at, size in column_chunks(D, WIN):
        v_t[at : at + size, :] = mm_nt(eye[:size, :size], values[:, at : at + size])
    whole(0)
    for at, size in column_chunks(D, CHUNK):
        for g in range(2):
            rows = x[g * 16 : g * 16 + 16].reshape(S, D)
            query[g * S : g * S + S, at : at + size] = mm(rows, w[0, :, at : at + size]).astype(BF16)
    valid = lax.broadcasted_iota(jnp.int32, (SLOTS, T), 0) < length
    for head in range(H):
        at = window(head)
        masked = keys[:, at : at + WIN] * lane_mask(head, at, WIN)
        scores = mm_nt(masked, query[:, at : at + WIN])
        expo, over[head] = softmax_cols(jnp.where(valid, scores, -1e30))
        weights[head] = expo.astype(BF16)
    for head in range(H):
        mine = slice(head * HEAD, head * HEAD + HEAD)
        ctx_t[mine, :] = mm(v_t[mine, :].astype(BF16), weights[head]) * over[head]
    for g in range(2):
        rows = slice(g * S, g * S + S)
        ctx[rows, :] = mm_nt(eye, ctx_t[:, rows].astype(BF16)).astype(BF16)
    whole(1)
    for at, size in column_chunks(D, WIN):
        cols = slice(at, at + size)
        for g in range(2):
            value = x[g * 16 : g * 16 + 16, :, cols].astype(F32).reshape(S, size)
            value = value + mm(ctx[g * S : g * S + S, :], w[1, :, cols])
            value = value.reshape(16, 2, 8, size)
            for f in range(2):
                out[f, g * 128 : g * 128 + 128, cols] = value[:, f].reshape(128, size).astype(BF16)


def vmem(*shape):
    return pltpu.VMEM(shape, BF16)


def weight_scratch():
    n = len(column_chunks(3 * D, CHUNK))
    return [
        vmem(D, 3 * D),
        vmem(D, D),
        pltpu.SemaphoreType.DMA,
        pltpu.SemaphoreType.DMA((n,)),
    ]


def call(kernel, name, shape, scratch, mebibytes, flops, transcendentals, spaces, *args):
    args = [
        pltpu.with_memory_space_constraint(arg, space) if space == pltpu.HBM else arg
        for arg, space in zip(args, spaces)
    ]
    return pl.pallas_call(
        kernel,
        out_shape=jax.ShapeDtypeStruct(shape, BF16),
        in_specs=[pl.BlockSpec(memory_space=pl.ANY if space == pltpu.HBM else space) for space in spaces],
        out_specs=pl.BlockSpec(memory_space=pltpu.VMEM),
        scratch_shapes=scratch,
        compiler_params=pltpu.CompilerParams(vmem_limit_bytes=mebibytes * 1024 * 1024),
        cost_estimate=pl.CostEstimate(
            flops=flops, bytes_accessed=13_000_000, transcendentals=transcendentals
        ),
        name=name,
    )(*args)


def spatial(*args):
    scratch = [vmem(T, D), vmem(T, 3 * D), vmem(H, S, S), vmem(T, D)]
    scratch = scratch + weight_scratch()
    spaces = [pltpu.VMEM, pltpu.VMEM, pltpu.HBM, pltpu.HBM]
    return call(spatial_kernel, "spatial", (32, 16, D), scratch, 22, 8_000_000_000, 2_100_000, spaces, *args)


def temporal(*args):
    scratch = [
        vmem(T, D),
        vmem(T, 3 * D),
        vmem(H, S, S),
        vmem(T, D),
        vmem(T, D),
        pltpu.VMEM((H, 1, S), F32),
        pltpu.VMEM((D, S), F32),
        pltpu.VMEM((D, S), F32),
        pltpu.VMEM((LANES, T + 8, 128), F32),
    ]
    scratch = scratch + weight_scratch()
    spaces = [pltpu.VMEM, pltpu.VMEM, pltpu.HBM, pltpu.HBM]
    return call(temporal_kernel, "temporal", (32, 16, D), scratch, 28, 8_000_000_000, 600_000, spaces, *args)


def cross(place, x, keys, values, pieces):
    scratch = [
        vmem(2, D, D),
        vmem(T, D),
        vmem(H, SLOTS, T),
        pltpu.VMEM((H, 1, T), F32),
        pltpu.VMEM((D, SLOTS), F32),
        pltpu.VMEM((D, T), F32),
        vmem(T, D),
        pltpu.SemaphoreType.DMA((2,)),
    ]
    args = (place, x, keys, values, *pieces)
    spaces = [pltpu.SMEM] + [pltpu.VMEM] * 3 + [pltpu.HBM] * len(pieces)
    return call(cross_kernel, "cross", (2, S, D), scratch, 16, 4_000_000_000, 1_000_000, spaces, *args)


def shift(array, axes, by, size):
    return lax.ppermute(array, axes, [(i, (i + by) % size) for i in range(size)])


def gather_even(first, last):
    shape = (8,) + first.shape
    copies = jnp.where(
        lax.axis_index("core") == 0,
        jnp.broadcast_to(first[None], shape),
        jnp.broadcast_to(last[None], shape),
    )
    return lax.all_to_all(copies, ("x_hi", "y"), split_axis=0, concat_axis=0, tiled=True)


def over_core(block):
    return shift(block, "core", 1, 2)


def over_z(block):
    return lax.ppermute(block, ("z_lo", "z_hi"), [(i, 3 - i) for i in range(4)])


def body(
    latent,
    modulation,
    w_spatial_qkv,
    w_spatial_out,
    w_temporal_qkv,
    w_temporal_out,
    cross_query,
    cross_out,
    text_keys,
    text_values,
    text_len,
):
    found = gather_even(cross_query, cross_out)
    after_spatial = spatial(latent.reshape(T, D), modulation, w_spatial_qkv, w_spatial_out)
    found, after_spatial = lax.optimization_barrier((found, after_spatial))
    placed = lax.all_to_all(after_spatial, SEQ, split_axis=0, concat_axis=0, tiled=True)
    own = [found[:4].reshape(BLOCK, D), found[4:].reshape(BLOCK, D)]
    others = [over_z(block) for block in own]
    own_swapped = [over_core(block) for block in own]
    own, own_swapped, others, placed = lax.optimization_barrier((own, own_swapped, others, placed))
    sides = [shift(own[n], ("x_hi", "x_lo"), (1, -1)[n], 4) for n in range(2)]
    far_side = shift(others[0], ("x_hi", "x_lo"), 1, 4)
    after_temporal = temporal(placed, modulation, w_temporal_qkv, w_temporal_out)
    sides, far_side, after_temporal = lax.optimization_barrier((sides, far_side, after_temporal))
    returned = lax.all_to_all(after_temporal, SEQ, split_axis=0, concat_axis=0, tiled=True)
    later = others + sides + [far_side, over_z(sides[1])]
    pieces = own + later + own_swapped + [over_core(block) for block in later]
    place = jnp.stack(
        [text_len[0], lax.axis_index("core"), lax.axis_index("z_lo"), lax.axis_index("x_lo")]
    ).astype(jnp.int32)
    fill = ((0, SLOTS - text_keys.shape[0]), (0, 0))
    keys, values = jnp.pad(text_keys, fill), jnp.pad(text_values, fill)
    return cross(place, returned, keys, values, pieces)


def solution(mesh):
    fine = Mesh(mesh.devices.reshape(2, 2, 2, 4, 2, 2), SEQ + ("z_hi", "core"))
    part = ("z_hi", "core")
    placed = (
        P(ALL, None, None),
        P(part, None),
        P(),
        P(),
        P(),
        P(),
        P(SEQ, None),
        P(SEQ, None),
        P(part, None),
        P(part, None),
        P(part),
    )
    return jax.shard_map(
        body, mesh=fine, in_specs=placed, out_specs=P(ALL, None, None), check_vma=False
    )
```

```python
import jax
import jax.numpy as jnp
import numpy as np
from jax import lax
from jax.experimental import pallas as pl
from jax.experimental.pallas import tpu as pltpu
from jax.sharding import Mesh, PartitionSpec as P

H = 16
HEAD = 72
LANES = 9
D = 1152
S = 256
T = 512
WIN = 256
SLOTS = 128
BLOCK = 144
CHUNK = 768
EXP_SCALE = float(np.log2(np.e) / np.sqrt(72.0))
F32 = jnp.float32
BF16 = jnp.bfloat16
NT = (((1,), (1,)), ((), ()))
SEQ = ("z_lo", "x_hi", "x_lo", "y")
ALL = ("z_hi", "core") + SEQ


def mm(a, b):
    return jnp.dot(a, b, preferred_element_type=F32)


def mm_nt(a, b):
    return lax.dot_general(a, b, NT, preferred_element_type=F32)


def window(head):
    return min(HEAD * head // 128 * 128, D - WIN)


def lane_mask(head, at, size):
    lane = lax.broadcasted_iota(jnp.int32, (1, size), 1) + at
    inside = (lane >= HEAD * head) & (lane < HEAD * head + HEAD)
    return jnp.where(inside, 1.0, 0.0).astype(BF16)


def heads_of(at, size):
    return [h for h in range(H) if h * HEAD < at + size and h * HEAD + HEAD > at]


def identity(n):
    rows = lax.broadcasted_iota(jnp.int32, (n, n), 0)
    cols = lax.broadcasted_iota(jnp.int32, (n, n), 1)
    return jnp.where(rows == cols, 1.0, 0.0).astype(BF16)


def norm_mod(values, shift, scale):
    mean = jnp.mean(values, axis=-1, keepdims=True)
    centered = values - mean
    var = jnp.mean(centered * centered, axis=-1, keepdims=True)
    return (centered * lax.rsqrt(var + 1e-06) * (1.0 + scale) + shift).astype(BF16)


def column_chunks(width, chunk):
    return [(at, min(chunk, width - at)) for at in range(0, width, chunk)]


def halves(body):
    for rows in (slice(0, S), slice(S, T)):
        body(rows)


def fetch(src, dst, sems):
    copies = []
    for n, (at, size) in enumerate(column_chunks(src.shape[1], CHUNK)):
        cols = pl.ds(at, size)
        copies.append(pltpu.make_async_copy(src.at[:, cols], dst.at[:, cols], sems.at[n]))
        copies[-1].start()
    return copies


def project_qkv(xn, w, copies, qkv):
    for copy, (at, size) in zip(copies, column_chunks(3 * D, CHUNK)):
        copy.wait()
        for rows in (slice(0, S), slice(S, T)):
            qkv[rows, at : at + size] = mm(xn[rows, :], w[:, at : at + size]).astype(BF16)


def softmax_rows(scores):
    top = jnp.max(scores, axis=1, keepdims=True)
    expo = jnp.exp2(scores * EXP_SCALE - top * EXP_SCALE)
    return (expo * (1.0 / jnp.sum(expo, axis=1, keepdims=True))).astype(BF16)


def softmax_cols(scores):
    top = jnp.max(scores, axis=0, keepdims=True)
    expo = jnp.exp2(scores * EXP_SCALE - top * EXP_SCALE)
    return expo, 1.0 / jnp.sum(expo, axis=0, keepdims=True)


def softmax_blocks(scores):
    low = lax.broadcasted_iota(jnp.int32, (64, 128), 1) < 64
    left, over_left = softmax_cols(jnp.where(low, scores[0:64, :128], scores[64:128, :128]))
    right, over_right = softmax_cols(jnp.where(low, scores[128:192, 128:], scores[192:256, 128:]))
    zero = jnp.zeros((64, 128), F32)
    wide = jnp.concatenate(
        [
            jnp.concatenate([jnp.where(low, left, zero), zero], 1),
            jnp.concatenate([jnp.where(low, zero, left), zero], 1),
            jnp.concatenate([zero, jnp.where(low, right, zero)], 1),
            jnp.concatenate([zero, jnp.where(low, zero, right)], 1),
        ],
        0,
    )
    return wide.astype(BF16), jnp.concatenate([over_left, over_right], 1)


def spatial_kernel(lat, mod, w_hbm, wo_hbm, out, xn, qkv, weights, ctx, w, wo, sem, wsems):
    copies = fetch(w_hbm, w, wsems)
    last = pltpu.make_async_copy(wo_hbm, wo, sem)
    last.start()
    shift, scale, gate = mod[0:1, :], mod[1:2, :], mod[2:3, :]

    def norm_rows(i, carry):
        rows = pl.ds(pl.multiple_of(i * 64, 64), 64)
        xn[rows, :] = norm_mod(lat[rows, :].astype(F32), shift, scale)
        return carry

    lax.fori_loop(0, T // 64, norm_rows, 0, unroll=4)
    project_qkv(xn, w, copies, qkv)

    def attend(rows):
        for head in range(H):
            at = window(head)
            query = qkv[rows, at : at + WIN] * lane_mask(head, at, WIN)
            weights[head] = softmax_rows(mm_nt(query, qkv[rows, D + at : D + at + WIN]))
        for at, size in column_chunks(D, WIN):
            values = qkv[rows, 2 * D + at : 2 * D + at + size]
            mixed = 0
            for head in heads_of(at, size):
                mixed = mixed + mm(weights[head], values * lane_mask(head, at, size))
            ctx[rows, at : at + size] = mixed.astype(BF16)

    halves(attend)
    last.wait()
    for at, size in column_chunks(D, WIN):
        cols = slice(at, at + size)
        parts = []
        for rows in (slice(0, S), slice(S, T)):
            value = lat[rows, cols].astype(F32) + gate[:, cols] * mm(ctx[rows, :], wo[:, cols])
            parts.append(value.reshape(32, 8, size))
        out[:, :, cols] = jnp.concatenate(parts, axis=1).astype(BF16)


def temporal_kernel(
    x, mod, w_hbm, wo_hbm, out, xn, qkv, weights, ctx, rest, over, v_t, ctx_t, wide, w, wo, sem, wsems
):
    copies = fetch(w_hbm, w, wsems)
    last = pltpu.make_async_copy(wo_hbm, wo, sem)
    last.start()
    shift, scale, gate = mod[3:4, :], mod[4:5, :], mod[5:6, :]

    def widen(i, carry):
        value = x[i].astype(F32)
        for j in range(LANES):
            wide[j, pl.ds(pl.multiple_of(i * 16, 16), 16), :] = value[:, j * 128 : j * 128 + 128]
        return carry

    lax.fori_loop(0, 32, widen, 0, unroll=4)

    def norm_rows(p, carry):
        picked = pl.ds(p, 64, stride=8)
        values = jnp.concatenate([wide[j, picked, :] for j in range(LANES)], axis=1)
        rows = pl.ds(pl.multiple_of(p * 64, 64), 64)
        rest[rows, :] = values.astype(BF16)
        xn[rows, :] = norm_mod(values, shift, scale)
        return carry

    lax.fori_loop(0, 8, norm_rows, 0, unroll=4)
    project_qkv(xn, w, copies, qkv)
    eye = identity(WIN)

    def attend(rows):
        for at, size in column_chunks(D, WIN):
            v_t[at : at + size, :] = mm_nt(eye[:size, :size], qkv[rows, 2 * D + at : 2 * D + at + size])
        for head in range(H):
            at = window(head)
            query = qkv[rows, at : at + WIN] * lane_mask(head, at, WIN)
            weights[head], over[head] = softmax_blocks(mm_nt(qkv[rows, D + at : D + at + WIN], query))
        for head in range(H):
            mine = slice(head * HEAD, head * HEAD + HEAD)
            ctx_t[mine, :] = mm(v_t[mine, :].astype(BF16), weights[head]) * over[head]
        ctx[rows, :] = mm_nt(eye, ctx_t[...].astype(BF16)).astype(BF16)

    halves(attend)
    last.wait()
    for at, size in column_chunks(D, WIN):
        cols = slice(at, at + size)
        for g in range(2):
            rows = slice(g * S, g * S + S)
            value = rest[rows, cols].astype(F32) + gate[:, cols] * mm(ctx[rows, :], wo[:, cols])
            for p in range(4):
                for j in range(size // 128):
                    piece = value[p * 64 : p * 64 + 64, j * 128 : j * 128 + 128]
                    wide[at // 128 + j, pl.ds(g * 4 + p, 64, stride=8), :] = piece

    def narrow(i, carry):
        rows = pl.ds(pl.multiple_of(i * 16, 16), 16)
        out[i] = jnp.concatenate([wide[j, rows, :] for j in range(LANES)], axis=1).astype(BF16)
        return carry

    lax.fori_loop(0, 32, narrow, 0, unroll=4)


def cross_kernel(place, x, keys, values, *refs):
    pieces, (out, w, query, weights, over, v_t, ctx_t, ctx, sems) = refs[:16], refs[16:]
    length, core, z_lo, x_lo = place[0], place[1], place[2], place[3]

    def put_whole(which, source):
        for n, src in enumerate(pieces[8 * source : 8 * source + 8]):
            x_hi, side, z = n % 2, n // 4, n // 2 % 2
            x = 2 * x_hi + (x_lo if side == 0 else 1 - x_lo)
            row = (z_lo if z == 0 else 1 - z_lo) * (D // 2) + x * BLOCK
            rows = pl.ds(pl.multiple_of(row, 16), BLOCK)
            pltpu.make_async_copy(src, w.at[which, rows, :], sems.at[which]).start()

    for one in range(2):

        @pl.when(core == one)
        def _():
            put_whole(0, one)
            put_whole(1, 1 - one)

    def whole(which):
        pltpu.make_async_copy(w.at[which], w.at[which], sems.at[which]).wait()

    eye = identity(WIN)
    for at, size in column_chunks(D, WIN):
        v_t[at : at + size, :] = mm_nt(eye[:size, :size], values[:, at : at + size])
    whole(0)
    for at, size in column_chunks(D, CHUNK):
        for g in range(2):
            rows = x[g * 16 : g * 16 + 16].reshape(S, D)
            query[g * S : g * S + S, at : at + size] = mm(rows, w[0, :, at : at + size]).astype(BF16)
    valid = lax.broadcasted_iota(jnp.int32, (SLOTS, T), 0) < length
    for head in range(H):
        at = window(head)
        masked = keys[:, at : at + WIN] * lane_mask(head, at, WIN)
        scores = mm_nt(masked, query[:, at : at + WIN])
        expo, over[head] = softmax_cols(jnp.where(valid, scores, -1e30))
        weights[head] = expo.astype(BF16)
    for head in range(H):
        mine = slice(head * HEAD, head * HEAD + HEAD)
        ctx_t[mine, :] = mm(v_t[mine, :].astype(BF16), weights[head]) * over[head]
    for g in range(2):
        rows = slice(g * S, g * S + S)
        ctx[rows, :] = mm_nt(eye, ctx_t[:, rows].astype(BF16)).astype(BF16)
    whole(1)
    for at, size in column_chunks(D, WIN):
        cols = slice(at, at + size)
        for g in range(2):
            value = x[g * 16 : g * 16 + 16, :, cols].astype(F32).reshape(S, size)
            value = value + mm(ctx[g * S : g * S + S, :], w[1, :, cols])
            value = value.reshape(16, 2, 8, size)
            for f in range(2):
                out[f, g * 128 : g * 128 + 128, cols] = value[:, f].reshape(128, size).astype(BF16)


def vmem(*shape):
    return pltpu.VMEM(shape, BF16)


def weight_scratch():
    n = len(column_chunks(3 * D, CHUNK))
    return [
        vmem(D, 3 * D),
        vmem(D, D),
        pltpu.SemaphoreType.DMA,
        pltpu.SemaphoreType.DMA((n,)),
    ]


def call(kernel, name, shape, scratch, mebibytes, flops, transcendentals, spaces, *args):
    args = [
        pltpu.with_memory_space_constraint(arg, space) if space == pltpu.HBM else arg
        for arg, space in zip(args, spaces)
    ]
    return pl.pallas_call(
        kernel,
        out_shape=jax.ShapeDtypeStruct(shape, BF16),
        in_specs=[pl.BlockSpec(memory_space=pl.ANY if space == pltpu.HBM else space) for space in spaces],
        out_specs=pl.BlockSpec(memory_space=pltpu.VMEM),
        scratch_shapes=scratch,
        compiler_params=pltpu.CompilerParams(vmem_limit_bytes=mebibytes * 1024 * 1024),
        cost_estimate=pl.CostEstimate(
            flops=flops, bytes_accessed=13_000_000, transcendentals=transcendentals
        ),
        name=name,
    )(*args)


def spatial(*args):
    scratch = [vmem(T, D), vmem(T, 3 * D), vmem(H, S, S), vmem(T, D)]
    scratch = scratch + weight_scratch()
    spaces = [pltpu.VMEM, pltpu.VMEM, pltpu.HBM, pltpu.HBM]
    return call(spatial_kernel, "spatial", (32, 16, D), scratch, 22, 8_000_000_000, 2_100_000, spaces, *args)


def temporal(*args):
    scratch = [
        vmem(T, D),
        vmem(T, 3 * D),
        vmem(H, S, S),
        vmem(T, D),
        vmem(T, D),
        pltpu.VMEM((H, 1, S), F32),
        pltpu.VMEM((D, S), F32),
        pltpu.VMEM((D, S), F32),
        pltpu.VMEM((LANES, T + 8, 128), F32),
    ]
    scratch = scratch + weight_scratch()
    spaces = [pltpu.VMEM, pltpu.VMEM, pltpu.HBM, pltpu.HBM]
    return call(temporal_kernel, "temporal", (32, 16, D), scratch, 28, 8_000_000_000, 600_000, spaces, *args)


def cross(place, x, keys, values, pieces):
    scratch = [
        vmem(2, D, D),
        vmem(T, D),
        vmem(H, SLOTS, T),
        pltpu.VMEM((H, 1, T), F32),
        pltpu.VMEM((D, SLOTS), F32),
        pltpu.VMEM((D, T), F32),
        vmem(T, D),
        pltpu.SemaphoreType.DMA((2,)),
    ]
    args = (place, x, keys, values, *pieces)
    spaces = [pltpu.SMEM] + [pltpu.VMEM] * 3 + [pltpu.HBM] * len(pieces)
    return call(cross_kernel, "cross", (2, S, D), scratch, 16, 4_000_000_000, 1_000_000, spaces, *args)


def shift(array, axes, by, size):
    return lax.ppermute(array, axes, [(i, (i + by) % size) for i in range(size)])


def gather_even(first, last):
    shape = (8,) + first.shape
    copies = jnp.where(
        lax.axis_index("core") == 0,
        jnp.broadcast_to(first[None], shape),
        jnp.broadcast_to(last[None], shape),
    )
    return lax.all_to_all(copies, ("x_hi", "y"), split_axis=0, concat_axis=0, tiled=True)


def over_core(block):
    return shift(block, "core", 1, 2)


def over_z(block):
    return lax.ppermute(block, ("z_lo", "z_hi"), [(i, 3 - i) for i in range(4)])


def body(
    latent,
    modulation,
    w_spatial_qkv,
    w_spatial_out,
    w_temporal_qkv,
    w_temporal_out,
    cross_query,
    cross_out,
    text_keys,
    text_values,
    text_len,
):
    found = gather_even(cross_query, cross_out)
    after_spatial = spatial(latent.reshape(T, D), modulation, w_spatial_qkv, w_spatial_out)
    found, after_spatial = lax.optimization_barrier((found, after_spatial))
    placed = lax.all_to_all(after_spatial, SEQ, split_axis=0, concat_axis=0, tiled=True)
    own = [found[:4].reshape(BLOCK, D), found[4:].reshape(BLOCK, D)]
    others = [over_z(block) for block in own]
    own_swapped = [over_core(block) for block in own]
    own, own_swapped, others, placed = lax.optimization_barrier((own, own_swapped, others, placed))
    sides = [shift(own[n], ("x_hi", "x_lo"), (1, -1)[n], 4) for n in range(2)]
    far_side = shift(others[0], ("x_hi", "x_lo"), 1, 4)
    after_temporal = temporal(placed, modulation, w_temporal_qkv, w_temporal_out)
    sides, far_side, after_temporal = lax.optimization_barrier((sides, far_side, after_temporal))
    returned = lax.all_to_all(after_temporal, SEQ, split_axis=0, concat_axis=0, tiled=True)
    later = others + sides + [far_side, over_z(sides[1])]
    pieces = own + later + own_swapped + [over_core(block) for block in later]
    place = jnp.stack(
        [text_len[0], lax.axis_index("core"), lax.axis_index("z_lo"), lax.axis_index("x_lo")]
    ).astype(jnp.int32)
    fill = ((0, SLOTS - text_keys.shape[0]), (0, 0))
    keys, values = jnp.pad(text_keys, fill), jnp.pad(text_values, fill)
    return cross(place, returned, keys, values, pieces)


def solution(mesh):
    fine = Mesh(mesh.devices.reshape(2, 2, 2, 4, 2, 2), SEQ + ("z_hi", "core"))
    part = ("z_hi", "core")
    placed = (
        P(ALL, None, None),
        P(part, None),
        P(),
        P(),
        P(),
        P(),
        P(SEQ, None),
        P(SEQ, None),
        P(part, None),
        P(part, None),
        P(part),
    )
    return jax.shard_map(
        body, mesh=fine, in_specs=placed, out_specs=P(ALL, None, None), check_vma=False
    )
```
